512 devices in a mesh: dp: 64 (over x, z), mp: 8 (over y, core).
Axes of the slice: x: 4, y: 4, z: 16, core: 2. Of those that a mesh axis runs over, the one named last changes fastest.
Arguments:
- checkpoint: bfloat16 [65536, 8192], P('dp', 'mp')
- key_grads: bfloat16 [65536, 1024], P('dp', 'mp'), may hold values from -16 to 16
- key_weight: bfloat16 [1024, 8192], P('dp', 'mp'), may hold values from -0.1875 to 0.1875
- norm_gain: float32 [8192], P('mp'), may hold values from 0.25 to 1.75
- picked_rows: int32 [64, 1024], P('dp'), may hold values from 0 to 1023, as said below
- row_counts: int32 [64], P('dp'), may hold values from 1 to 1024, as said below
Outputs:
- row_grads: bfloat16 [65536, 8192], P('dp', 'mp')
- weight_grad: float32 [1024, 8192], P('dp', 'mp')
- gain_grad: float32 [8192], P('mp')
The draws below stay inside these ranges and needn't reach their ends.
Inputs may be any that keep to these rules, and one draw needn't show every extreme that they name: `picked_rows`: only the first row_counts[s] entries of row s are used; the entries of a row are distinct. `row_counts`: the counts sum to exactly 8192; one index of dp has exactly 1024, another exactly 1.
All inputs are finite; a program needn't handle non-finite values.
Results may differ from the reference program's by a relative error of at most 0.0029.
Values may be sent and summed in bfloat16 or wider, within the bound.
A program may use at most 64 MiB of HBM per device.

```python
import jax
import jax.numpy as jnp
from jax import lax

D = 8192
KVW = 1024
TOK_DEV = 1024
SEL_DEV = 128
CAP = 1024
TOKENS = 65536
N_DP = 64


def draw_checkpoint(key, part):
    key = jax.random.fold_in(key, 11)
    first, second = jax.random.split(key)
    position = jnp.arange(D, dtype=jnp.float32) / D
    values = jax.random.normal(first, (TOKENS, D), jnp.float32)
    column = jnp.exp(jnp.log(2.0) * position)
    scales = jnp.exp(jax.random.uniform(second, (TOKENS, 1), jnp.float32, jnp.log(0.4), jnp.log(4.0)))
    return (values * column[None, :] * scales).astype(jnp.bfloat16)


def draw_picked_rows(key, part):
    key = jax.random.fold_in(key, 7)
    keys = jax.random.split(key, N_DP)
    return jax.vmap(lambda single: jax.random.permutation(single, TOK_DEV)[:CAP])(keys).astype(jnp.int32)


def draw_row_counts(key, part):
    key = jax.random.fold_in(key, 5)
    first, second, third = jax.random.split(key, 3)
    fullest = jax.random.randint(first, (), 0, N_DP)
    weights = jax.random.randint(second, (N_DP - 1,), 1, 5)
    lightest = jax.random.randint(third, (), 0, N_DP - 1)
    weights = jnp.where(jnp.arange(N_DP - 1) == lightest, 0, weights)
    rest = SEL_DEV * N_DP - CAP - (N_DP - 1)
    running = jnp.cumsum(weights)
    edges = rest * running // running[-1]
    before = jnp.concatenate([jnp.zeros((1,), jnp.int32), edges[:-1].astype(jnp.int32)])
    others = 1 + edges.astype(jnp.int32) - before
    places = jnp.arange(N_DP)
    spots = jnp.clip(places - (places > fullest).astype(jnp.int32), 0, N_DP - 2)
    return jnp.where(places == fullest, CAP, jnp.take(others, spots)).astype(jnp.int32)


def strengthened(entries, key, source, target, blocks, factor):
    def block_of(dim):
        return (jnp.arange(entries.shape[dim]) // (entries.shape[dim] // blocks)).reshape((-1,) + (1,) * (entries.ndim - 1 - dim))

    near = jax.random.permutation(key, blocks)[block_of(target)]
    second = (block_of(target) + blocks // 2) % blocks
    return jnp.where((block_of(source) == near) | (block_of(source) == second), factor * entries, entries)


def shard_levels(key, shape, pieces, smallest, largest):
    level, own = 1.0, jax.random.fold_in(key, 6)
    for dim, shards_of in pieces:
        steps = jnp.exp(jax.random.uniform(jax.random.fold_in(own, dim), (shards_of,), jnp.float32, smallest / len(pieces), largest / len(pieces)))
        level = level * jnp.repeat(steps, shape[dim] // shards_of).reshape([-1 if axis == dim else 1 for axis in range(len(shape))])
    return level


def bell_draw(own_key, dims, spread, bound, shards=(), held_as=jnp.bfloat16):
    gain = shard_levels(own_key, dims, shards, -0.22, 0.18) if shards else 1.0
    result = jax.random.normal(own_key, dims, jnp.float32) * spread * gain
    return jnp.minimum(jnp.maximum(result, -bound), bound).astype(held_as)


def heavy_noise(own_key, shape, deviation, bound, cuts, heavy, kind=jnp.bfloat16):
    result = deviation * jax.random.normal(own_key, shape, jnp.float32)
    if cuts:
        result = result * shard_levels(own_key, shape, cuts, -0.22, 0.18)
    return jnp.clip(strengthened(result, jax.random.fold_in(own_key, 3), *heavy), -bound, bound).astype(kind)


def setup_inputs(seed: int = 0) -> dict:
    streams_of = jax.random.split(jax.random.key(seed), 7)
    return {
        "checkpoint": draw_checkpoint(jax.random.fold_in(streams_of[6], 71), 0),
        "key_grads": heavy_noise(streams_of[1], (TOKENS, KVW), 1.0, 16.0, ((0, 64), (1, 8)), (0, 1, 64, 4.0)),
        "key_weight": bell_draw(streams_of[2], (KVW, D), KVW ** -0.5, 0.1875, ((0, 64), (1, 8))),
        "norm_gain": jnp.clip(1.0 + 0.15 * jax.random.normal(streams_of[3], (D,), jnp.float32), 0.25, 1.75),
        "picked_rows": draw_picked_rows(jax.random.fold_in(streams_of[6], 71), 0),
        "row_counts": draw_row_counts(jax.random.fold_in(streams_of[6], 71), 0),
    }


epsilon = 1e-05

def reference(checkpoint, key_grads, key_weight, norm_gain, picked_rows, row_counts):
    gain_f = norm_gain.astype(jnp.float32)

    def handle(carry, index):
        weight_sum, gain_sum = carry
        row_ids = lax.dynamic_slice_in_dim(picked_rows, index, 1, 0)[0].astype(jnp.int32)
        whole_ids = (index * TOK_DEV + row_ids).astype(jnp.int32)
        live = jnp.arange(CAP, dtype=jnp.int32) < row_counts[index]
        rows = jnp.take(checkpoint, whole_ids, axis=0).astype(jnp.float32)
        cot = jnp.take(key_grads, whole_ids, axis=0)
        cot = jnp.where(live[:, None], cot, jnp.zeros((), jnp.bfloat16))
        inverse = lax.rsqrt(lax.optimization_barrier(jnp.sum(rows * rows, axis=1)) / D + epsilon)
        normed = rows * inverse[:, None]
        hidden = (normed * gain_f).astype(jnp.bfloat16)
        grad_hidden = jnp.dot(cot, key_weight, preferred_element_type=jnp.float32)
        scaled = gain_f * grad_hidden
        inner = lax.optimization_barrier(jnp.sum(scaled * normed, axis=1))
        grads = inverse[:, None] * (scaled - normed * (inner[:, None] / D))
        grads = jnp.where(live[:, None], grads, jnp.zeros((), jnp.float32)).astype(jnp.bfloat16)
        weight_sum = weight_sum + jnp.dot(jnp.transpose(cot), hidden, preferred_element_type=jnp.float32)
        gain_sum = gain_sum + lax.optimization_barrier(jnp.sum(grad_hidden * normed, axis=0))
        return ((weight_sum, gain_sum), grads)
    start = (jnp.zeros((KVW, D), jnp.float32), jnp.zeros((D,), jnp.float32))
    (weight_grad, gain_grad), row_grads = lax.scan(handle, start, jnp.arange(N_DP, dtype=jnp.int32))
    return (row_grads.reshape(N_DP * CAP, D), weight_grad, gain_grad)
```

```python
import functools

import jax
import jax.numpy as jnp
from jax import lax
from jax.experimental import pallas as pl
from jax.experimental.pallas import tpu as pltpu
from jax.sharding import PartitionSpec as P

D = 8192
EPS = 1e-05
NX, NZ, NY = 4, 16, 4
MESH = pl.DeviceIdType.MESH
F32, BF16 = jnp.float32, jnp.bfloat16
ORDER = (0, 3, 1, 2)


def rem(a, n):
    return lax.rem(a, n)


def dot(a, b):
    return jnp.dot(a, b, preferred_element_type=F32)


def kernel(
    x_in, kg_in, w_in, gain, picked, count,
    rows_out, wg_out, gg_out,
    X, KG, GT, W, H, GH, RG, OUT,
    inv_c,
    SQ, IN, GX, GZ,
    S2, D1, D3, F1, F3, U1, U3, R,
    RA, RB, DA, DB, SA, SB, ZM, ZP,
    lsem, osem, ws, wr, wxs, wxr, ys, yr, sqs, sqr, ins, inr, gxs, gxr, gzs, gzr,
    xs, xr, zs, zr,
):
    dp, mp = lax.axis_index("dp"), lax.axis_index("mp")
    x, z = lax.div(dp, NZ), rem(dp, NZ)
    y, c = lax.div(mp, 2), rem(mp, 2)
    pending = []

    def to_x(k):
        return (rem(x + k, NX) * NZ + z, mp)

    def to_z(k):
        return (x * NZ + rem(z + k, NZ), mp)

    def to_y(k):
        return (dp, rem(y + k, NY) * 2 + c)

    def to_mp(k):
        return (dp, rem(mp + k, 8))

    sibling = (dp, 2 * y + 1 - c)

    def send(src, dst, ss, rs, dev):
        copy = pltpu.make_async_remote_copy(
            src_ref=src, dst_ref=dst, send_sem=ss, recv_sem=rs, device_id=dev, device_id_type=MESH
        )
        copy.start()
        pending.append(copy)

    def arrived(dst, ss, rs, dev):
        pltpu.make_async_remote_copy(
            src_ref=dst, dst_ref=dst, send_sem=ss, recv_sem=rs, device_id=dev, device_id_type=MESH
        ).wait_recv()

    get_kg = pltpu.make_async_copy(kg_in, KG, lsem.at[0])
    get_x = pltpu.make_async_copy(x_in, X, lsem.at[1])
    get_w = pltpu.make_async_copy(w_in, W.at[x, z], lsem.at[2])
    get_kg.start()
    get_w.start()
    get_x.start()

    barrier = pltpu.get_barrier_semaphore()
    for k in range(1, 8):
        pl.semaphore_signal(barrier, inc=1, device_id=to_mp(k), device_id_type=MESH)
    for k in range(1, NX):
        pl.semaphore_signal(barrier, inc=1, device_id=to_x(k), device_id_type=MESH)
    for k in range(1, NZ):
        pl.semaphore_signal(barrier, inc=1, device_id=to_z(k), device_id_type=MESH)
    pl.semaphore_wait(barrier, 7 + NX - 1 + NZ - 1)

    get_w.wait()
    for k in range(1, NX):
        send(W.at[x, z], W.at[x, z], wxs.at[k], wxr.at[k], to_x(k))

    get_kg.wait()

    def flip(j, _):
        rows = pl.ds(pl.multiple_of(j * 128, 128), 128)
        GT[mp, :, rows] = KG[rows, :].T
        return 0

    lax.fori_loop(0, 8, flip, 0)

    def block(k, other=False):
        return rem(y + k, NY) * 2 + ((1 - c) if other else c)

    def half(b, h):
        return GT.at[b, pl.ds(64 * h, 64), :]

    send(half(mp, 0), half(mp, 0), ys.at[1], yr.at[1], to_y(1))
    send(half(mp, 1), half(mp, 1), ys.at[3], yr.at[3], to_y(3))
    send(half(mp, 1), half(mp, 1), ys.at[2], yr.at[2], to_y(1))
    send(half(mp, 0), half(mp, 0), ys.at[4], yr.at[4], to_y(3))
    send(GT.at[mp], GT.at[mp], ys.at[0], yr.at[0], sibling)

    eye = lax.broadcasted_iota(jnp.int32, (128, 128), 0) == lax.broadcasted_iota(
        jnp.int32, (128, 128), 1
    )

    def to_row(col):
        return jnp.sum(jnp.where(eye, col, 0.0), axis=0, keepdims=True)

    def to_col(row):
        return jnp.sum(jnp.where(eye, row, 0.0), axis=1, keepdims=True)

    get_x.wait()

    def squares(j, _):
        rows = X[pl.ds(pl.multiple_of(j * 128, 128), 128), :].astype(F32)
        SQ[mp, pl.ds(j, 1), :] = to_row(jnp.sum(rows * rows, axis=1, keepdims=True))
        return 0

    lax.fori_loop(0, 8, squares, 0)
    for k in range(1, 8):
        send(SQ.at[mp], SQ.at[mp], sqs.at[k], sqr.at[k], to_mp(k))

    live = lax.broadcasted_iota(jnp.int32, (1, 1024), 1) < count[0]
    wanted = jnp.where(live, picked[...], -1)

    def selected(j, _):
        number = lax.broadcasted_iota(jnp.int32, (128, 1024), 0) + j * 128
        hit = jnp.where(wanted == number, 1.0, 0.0)
        inv_c[pl.ds(pl.multiple_of(j * 128, 128), 128), :] = jnp.sum(hit, axis=1, keepdims=True)
        return 0

    lax.fori_loop(0, 8, selected, 0)

    def w_part(zz, h):
        return W.at[:, rem(zz + 2 * NZ, NZ), :, pl.ds(512 * h, 512)]

    def w_ways(s, h):
        return [d for d in (0, 1) if s < 7 or d == h]

    def w_arrive(s, h):
        for d in w_ways(s, h):
            zz = z - 1 - s if d == 0 else z + 1 + s
            part = w_part(zz, h)
            arrived(part, ws.at[s, h, d], wr.at[s, h, d], to_z(15 if d == 0 else 1))

    def w_step(s):
        for h in (0, 1):
            if s > 0:
                w_arrive(s - 1, h)
            for d in w_ways(s, h):
                part = w_part(z - s if d == 0 else z + s, h)
                send(part, part, ws.at[s, h, d], wr.at[s, h, d], to_z(1 if d == 0 else 15))

    for k in range(1, NX):
        part = W.at[rem(x + NX - k, NX), z]
        arrived(part, wxs.at[k], wxr.at[k], to_x(NX - k))
    w_step(0)

    for k in range(1, 8):
        arrived(SQ.at[rem(mp + 8 - k, 8)], sqs.at[k], sqr.at[k], to_mp(8 - k))
    total = SQ[0]
    for k in range(1, 8):
        total = total + SQ[k]
    SQ[8] = lax.rsqrt(total / D + EPS)

    def hidden(j, _):
        rows = pl.ds(pl.multiple_of(j * 128, 128), 128)
        inverse = to_col(SQ[8, pl.ds(j, 1), :]) * inv_c[rows, :]
        inv_c[rows, :] = inverse
        normed = X[rows, :].astype(F32) * inverse
        H[rows, :] = (normed * gain[...]).astype(BF16)
        return 0

    lax.fori_loop(0, 8, hidden, 0)

    arrived(half(block(3), 0), ys.at[1], yr.at[1], to_y(3))
    send(half(block(3), 0), half(block(3), 0), ys.at[5], yr.at[5], to_y(1))
    arrived(half(block(1), 1), ys.at[3], yr.at[3], to_y(1))
    send(half(block(1), 1), half(block(1), 1), ys.at[6], yr.at[6], to_y(3))
    w_step(1)
    arrived(half(block(3), 1), ys.at[2], yr.at[2], to_y(3))
    send(GT.at[block(3)], GT.at[block(3)], ys.at[7], yr.at[7], sibling)
    arrived(half(block(1), 0), ys.at[4], yr.at[4], to_y(1))
    send(GT.at[block(1)], GT.at[block(1)], ys.at[8], yr.at[8], sibling)
    w_step(2)
    arrived(half(block(2), 0), ys.at[5], yr.at[5], to_y(3))
    arrived(half(block(2), 1), ys.at[6], yr.at[6], to_y(1))
    send(GT.at[block(2)], GT.at[block(2)], ys.at[9], yr.at[9], sibling)
    w_step(3)
    arrived(GT.at[block(0, True)], ys.at[0], yr.at[0], sibling)
    arrived(GT.at[block(3, True)], ys.at[7], yr.at[7], sibling)
    arrived(GT.at[block(1, True)], ys.at[8], yr.at[8], sibling)
    arrived(GT.at[block(2, True)], ys.at[9], yr.at[9], sibling)

    def terms(k, left, right):
        b = rem(x + k, NX)

        def tile(n, _):
            lhs = GT[pl.ds(2 * b, 2)].reshape(256, 1024)
            here = pl.ds(pl.multiple_of(n * 256, 256), 256)
            low = dot(lhs, H[:, here])
            left[:, :, here] = low.reshape(16, 16, 256).astype(left.dtype)
            there = pl.ds(pl.multiple_of(n * 256 + 512, 256), 256)
            high = dot(lhs, H[:, there])
            right[:, :, here] = high.reshape(16, 16, 256).astype(right.dtype)
            return 0

        lax.fori_loop(0, 2, tile, 0)

    def group(ref, j):
        g = rem(lax.div(z, 4) + 2 + ORDER[j], 4)
        return ref.at[pl.ds(4 * g, 4)]

    def x_send(i, j, src, dst, d):
        send(group(src, j), group(dst, j), xs.at[i, j, d], xr.at[i, j, d], to_x(1 if d == 0 else 3))

    def x_arrived(i, j, dst, d):
        arrived(group(dst, j), xs.at[i, j, d], xr.at[i, j, d], to_x(3 if d == 0 else 1))

    terms(2, S2.at[0], S2.at[1])
    for j in range(4):
        x_send(0, j, S2.at[0], RA, 0)
        x_send(0, j, S2.at[1], RB, 1)
    terms(1, F1, D1)
    for j in range(4):
        x_send(1, j, D1, DB, 0)
    terms(3, D3, F3)
    for j in range(4):
        x_send(1, j, D3, DA, 1)
    terms(0, R.at[0], R.at[1])

    def relay(j):
        x_arrived(0, j, RA, 0)
        group(U1, j)[...] = (group(F1, j)[...] + group(RA, j)[...].astype(F32)).astype(BF16)
        x_send(2, j, U1, SA, 0)
        x_arrived(0, j, RB, 1)
        group(U3, j)[...] = (group(F3, j)[...] + group(RB, j)[...].astype(F32)).astype(BF16)
        x_send(2, j, U3, SB, 1)

    def owned(j):
        x_arrived(1, j, DB, 0)
        x_arrived(1, j, DA, 1)
        x_arrived(2, j, SA, 0)
        x_arrived(2, j, SB, 1)
        for h, (first, second) in enumerate(((DA, SA), (DB, SB))):
            mine = group(R.at[h], j)
            mine[...] = mine[...] + group(first, j)[...].astype(F32) + group(second, j)[...].astype(F32)

    for s in range(4, 8):
        w_step(s)
        relay(s - 4)

    def z_arrived(s, h, d):
        buf = (ZM if d == 0 else ZP).at[h, s]
        arrived(buf, zs.at[s, h, d], zr.at[s, h, d], to_z(1 if d == 0 else 15))

    def z_step(s):
        for h in (0, 1):
            for d in (0, 1) if s < 7 else (0,):
                buf = ZM if d == 0 else ZP
                owner = rem(z + 8 + s if d == 0 else z + 16 + 7 - s, NZ)
                if s == 0:
                    src = R.at[h, owner]
                else:
                    z_arrived(s - 1, h, d)
                    src = buf.at[h, s - 1]
                    src[...] = src[...] + R[h, owner]
                send(src, buf.at[h, s], zs.at[s, h, d], zr.at[s, h, d], to_z(15 if d == 0 else 1))

    def backward(r):
        rows = pl.ds(256 * r, 256)
        lhs = GT[:, :, rows].reshape(1024, 256).T

        def tile(n, _):
            here = pl.ds(pl.multiple_of(n * 256, 256), 256)
            GH[rows, here] = dot(lhs, W[:, :, :, here].reshape(1024, 256))
            return 0

        lax.fori_loop(0, 4, tile, 0)
        for i in (0, 1):
            j = 2 * r + i
            part = pl.ds(128 * j, 128)
            normed = X[part, :].astype(F32) * inv_c[part, :]
            product = GH[part, :] * normed
            sums = jnp.sum(product, axis=0, keepdims=True)
            for b in range(8):
                piece = sums[:, 128 * b : 128 * b + 128]
                if j == 0:
                    GX[x, b : b + 1, :] = piece
                else:
                    GX[x, b : b + 1, :] = GX[x, b : b + 1, :] + piece
            inner = jnp.sum(gain[...] * product, axis=1, keepdims=True)
            IN[mp, j : j + 1, :] = to_row(inner)

    for h in (0, 1):
        w_arrive(7, h)
    owned(0)
    owned(1)
    z_step(0)
    backward(0)
    owned(2)
    z_step(1)
    backward(1)
    z_step(2)
    backward(2)
    z_step(3)
    backward(3)
    for k in range(1, 8):
        send(IN.at[mp], IN.at[mp], ins.at[k], inr.at[k], to_mp(k))
    for k in range(1, NX):
        send(GX.at[x], GX.at[x], gxs.at[k], gxr.at[k], to_x(k))
    owned(3)
    z_step(4)
    for k in range(1, 8):
        arrived(IN.at[rem(mp + 8 - k, 8)], ins.at[k], inr.at[k], to_mp(8 - k))
    total = IN[0]
    for k in range(1, 8):
        total = total + IN[k]
    IN[8] = total / D
    for k in range(1, NX):
        arrived(GX.at[rem(x + NX - k, NX)], gxs.at[k], gxr.at[k], to_x(NX - k))
    GZ[z] = GX[0] + GX[1] + GX[2] + GX[3]
    for k in range(1, NZ):
        send(GZ.at[z], GZ.at[z], gzs.at[k], gzr.at[k], to_z(k))

    def finish(j, _):
        rows = pl.ds(pl.multiple_of(j * 128, 128), 128)
        inner = to_col(IN[8, pl.ds(j, 1), :])
        inverse = inv_c[rows, :]
        normed = X[rows, :].astype(F32) * inverse
        RG[rows, :] = (inverse * (gain[...] * GH[rows, :] - normed * inner)).astype(BF16)
        return 0

    lax.fori_loop(0, 8, finish, 0)
    z_step(5)

    def place(r):
        def column(i):
            row = picked[:, 256 * r + 128 * i : 256 * r + 128 * i + 128].astype(F32)
            return to_col(row)

        ids = jnp.concatenate([column(0), column(1)], axis=0).astype(jnp.int32)
        slot = lax.broadcasted_iota(jnp.int32, (256, 1), 0) + 256 * r
        ids = jnp.where(slot < count[0], ids, -1)
        number = lax.broadcasted_iota(jnp.int32, (256, 1024), 1)
        choice = jnp.where(ids == number, 1.0, 0.0).astype(BF16)
        rows = pl.ds(256 * r, 256)

        def tile(n, _):
            here = pl.ds(pl.multiple_of(n * 256, 256), 256)
            OUT[rows, here] = dot(choice, RG[:, here]).astype(BF16)
            return 0

        lax.fori_loop(0, 4, tile, 0)
        copy = pltpu.make_async_copy(OUT.at[rows], rows_out.at[rows], osem.at[r])
        copy.start()
        return copy

    written = [place(0), place(1)]
    z_step(6)
    written += [place(2), place(3)]
    z_step(7)
    for k in range(1, NZ):
        arrived(GZ.at[rem(z + NZ - k, NZ)], gzs.at[k], gzr.at[k], to_z(NZ - k))
    total = GZ[0]
    for k in range(1, NZ):
        total = total + GZ[k]
    gg_out[...] = total
    for h in (0, 1):
        z_arrived(7, h, 0)
        z_arrived(6, h, 1)
        wg_out[:, 512 * h : 512 * h + 512] = R[h, z] + ZM[h, 7] + ZP[h, 6]
    for copy in written:
        copy.wait()
    for copy in pending:
        copy.wait_send()


def shards(checkpoint, key_grads, key_weight, norm_gain, picked_rows, row_counts):
    any_space = pl.BlockSpec(memory_space=pl.ANY)
    vmem = pl.BlockSpec(memory_space=pltpu.VMEM)
    smem = pl.BlockSpec(memory_space=pltpu.SMEM)
    dma = pltpu.SemaphoreType.DMA
    halfblock = (16, 16, 512)
    scratch = [
        pltpu.VMEM((1024, 1024), BF16),
        pltpu.VMEM((1024, 128), BF16),
        pltpu.VMEM((8, 128, 1024), BF16),
        pltpu.VMEM((NX, NZ, 16, 1024), BF16),
        pltpu.VMEM((1024, 1024), BF16),
        pltpu.VMEM((1024, 1024), F32),
        pltpu.VMEM((1024, 1024), BF16),
        pltpu.VMEM((1024, 1024), BF16),
        pltpu.VMEM((1024, 1), F32),
        pltpu.VMEM((9, 8, 128), F32),
        pltpu.VMEM((9, 8, 128), F32),
        pltpu.VMEM((NX, 8, 128), F32),
        pltpu.VMEM((NZ, 8, 128), F32),
        pltpu.VMEM((2,) + halfblock, BF16),
        pltpu.VMEM(halfblock, BF16),
        pltpu.VMEM(halfblock, BF16),
        pltpu.VMEM(halfblock, F32),
        pltpu.VMEM(halfblock, F32),
        pltpu.VMEM(halfblock, BF16),
        pltpu.VMEM(halfblock, BF16),
        pltpu.VMEM((2,) + halfblock, F32),
        *[pltpu.VMEM(halfblock, BF16) for _ in range(6)],
        pltpu.VMEM((2, 8, 16, 512), F32),
        pltpu.VMEM((2, 7, 16, 512), F32),
        dma((3,)), dma((4,)),
        dma((8, 2, 2)), dma((8, 2, 2)),
        dma((NX,)), dma((NX,)),
        dma((10,)), dma((10,)),
        dma((8,)), dma((8,)),
        dma((8,)), dma((8,)),
        dma((NX,)), dma((NX,)),
        dma((NZ,)), dma((NZ,)),
        dma((3, 4, 2)), dma((3, 4, 2)),
        dma((8, 2, 2)), dma((8, 2, 2)),
    ]
    row_grads, weight_grad, gain_grad = pl.pallas_call(
        kernel,
        out_shape=(
            jax.ShapeDtypeStruct((1024, 1024), BF16),
            jax.ShapeDtypeStruct((16, 1024), F32),
            jax.ShapeDtypeStruct((8, 128), F32),
        ),
        in_specs=[any_space, any_space, any_space, vmem, vmem, smem],
        out_specs=(any_space, vmem, vmem),
        scratch_shapes=scratch,
        compiler_params=pltpu.CompilerParams(
            collective_id=0, has_side_effects=True, vmem_limit_bytes=48 * 1024 * 1024
        ),
        cost_estimate=pl.CostEstimate(flops=6 * 1024**3, bytes_accessed=8 * 1024**2, transcendentals=1024),
        name="norm_key_backward",
    )(checkpoint, key_grads, key_weight, norm_gain.reshape(1, 1024), picked_rows, row_counts)
    return row_grads, weight_grad, gain_grad.reshape(1024)


def solution(mesh):
    in_specs = (P("dp", "mp"), P("dp", "mp"), P("dp", "mp"), P("mp"), P("dp", None), P("dp"))
    out_specs = (P("dp", "mp"), P("dp", "mp"), P("mp"))
    return jax.shard_map(shards, mesh=mesh, in_specs=in_specs, out_specs=out_specs, check_vma=False)
```

```python
import functools

import jax
import jax.numpy as jnp
from jax import lax
from jax.experimental import pallas as pl
from jax.experimental.pallas import tpu as pltpu
from jax.sharding import PartitionSpec as P

D = 8192
EPS = 1e-05
NX, NZ, NY = 4, 16, 4
MESH = pl.DeviceIdType.MESH
F32, BF16 = jnp.float32, jnp.bfloat16


def rem(a, n):
    return lax.rem(a, n)


def dot(a, b):
    return jnp.dot(a, b, preferred_element_type=F32)


def kernel(
    x_in, kg_in, w_in, gain_in, picked_in, count,
    rows_out, wg_out, gg_out,
    X, KG, GT, G, WR, W, H, GH, RG, OUT,
    gain, picked, inv_c,
    SQ, IN, GX, GZ,
    S2, D1, D3, F1, F3, U1, U3, R,
    RA, RB, DA, DB, SA, SB, QA, QR, T, TR,
    lsem, osem, ws, wr, ys, yr, sqs, sqr, ins, inr, gxs, gxr, gzs, gzr,
    xs, xr, qs, qr, ts, tr,
):
    dp, mp = lax.axis_index("dp"), lax.axis_index("mp")
    x, z = lax.div(dp, NZ), rem(dp, NZ)
    y, c = lax.div(mp, 2), rem(mp, 2)
    pending = []

    def to_x(k):
        return (rem(x + k, NX) * NZ + z, mp)

    def to_z(k):
        return (x * NZ + rem(z + k, NZ), mp)

    def to_y(k):
        return (dp, rem(y + k, NY) * 2 + c)

    def to_mp(k):
        return (dp, rem(mp + k, 8))

    sibling = (dp, 2 * y + 1 - c)

    def send(src, dst, ss, rs, dev):
        copy = pltpu.make_async_remote_copy(
            src_ref=src, dst_ref=dst, send_sem=ss, recv_sem=rs, device_id=dev, device_id_type=MESH
        )
        copy.start()
        pending.append(copy)

    def arrived(dst, ss, rs, dev):
        pltpu.make_async_remote_copy(
            src_ref=dst, dst_ref=dst, send_sem=ss, recv_sem=rs, device_id=dev, device_id_type=MESH
        ).wait_recv()

    get_kg = pltpu.make_async_copy(kg_in, KG, lsem.at[0])
    get_x = pltpu.make_async_copy(x_in, X, lsem.at[1])
    get_w = pltpu.make_async_copy(w_in, WR.at[0, 0, 0], lsem.at[2])
    get_gain = pltpu.make_async_copy(gain_in, gain, lsem.at[3])
    get_picked = pltpu.make_async_copy(picked_in, picked, lsem.at[4])
    get_kg.start()
    get_w.start()
    get_x.start()
    get_gain.start()
    get_picked.start()

    barrier = pltpu.get_barrier_semaphore()
    for k in range(1, NZ):
        pl.semaphore_signal(barrier, inc=1, device_id=to_z(k), device_id_type=MESH)
    for k in range(1, NX):
        pl.semaphore_signal(barrier, inc=1, device_id=to_x(k), device_id_type=MESH)
    for k in range(1, 8):
        pl.semaphore_signal(barrier, inc=1, device_id=to_mp(k), device_id_type=MESH)

    get_kg.wait()

    def flip(j, _):
        rows = pl.ds(pl.multiple_of(j * 128, 128), 128)
        GT[mp, :, rows] = KG[rows, :].T
        return 0

    lax.fori_loop(0, 8, flip, 0)
    get_w.wait()
    pl.semaphore_wait(barrier, 7 + NX - 1 + NZ - 1)

    whole, low, high = slice(None), pl.ds(0, 512), pl.ds(512, 512)
    later = pl.ds(1, 3)

    def w_send(i, src, dst, dev, cols=whole):
        send(WR.at[(*src, whole, cols)], WR.at[(*dst, whole, cols)], ws.at[i], wr.at[i], dev)

    def w_arrived(i, dst, cols=whole):
        arrived(WR.at[(*dst, whole, cols)], ws.at[i], wr.at[i], to_x(1))

    near = ((1, 15), (3, 1), (2, 14))

    def w_cross(i, j, m):
        w_send(i, (0, j, m), (1, j, m), to_x(3))
        w_send(i + 1, (0, j, m), (3, j, m), to_x(1))

    def w_relay(i, j, m):
        w_arrived(i, (1, j, m))
        w_send(i + 2, (1, j, m), (2, j, m), to_x(3), low)
        w_arrived(i + 1, (3, j, m))
        w_send(i + 3, (3, j, m), (2, j, m), to_x(1), high)

    def w_relayed(i, j, m):
        w_arrived(i + 2, (2, j, m), low)
        w_arrived(i + 3, (2, j, m), high)

    for i, (j, k) in enumerate(near):
        w_send(i, (0, 0, 0), (0, j, 0), to_z(k))
    w_cross(10, 0, 0)
    for m in (1, 3, 2):
        w_send(2 + m, (0, 0, 0), (0, 0, m), to_z(16 - 4 * m))

    def block(k, other=False):
        return rem(y + k, NY) * 2 + ((1 - c) if other else c)

    def half(b, h):
        return GT.at[b, pl.ds(64 * h, 64), :]

    send(half(mp, 0), half(mp, 0), ys.at[1], yr.at[1], to_y(1))
    send(half(mp, 1), half(mp, 1), ys.at[3], yr.at[3], to_y(3))
    send(half(mp, 1), half(mp, 1), ys.at[2], yr.at[2], to_y(1))
    send(half(mp, 0), half(mp, 0), ys.at[4], yr.at[4], to_y(3))
    send(GT.at[mp], GT.at[mp], ys.at[0], yr.at[0], sibling)

    eye = lax.broadcasted_iota(jnp.int32, (128, 128), 0) == lax.broadcasted_iota(
        jnp.int32, (128, 128), 1
    )

    def to_row(col):
        return jnp.sum(jnp.where(eye, col, 0.0), axis=0, keepdims=True)

    def to_col(row):
        return jnp.sum(jnp.where(eye, row, 0.0), axis=1, keepdims=True)

    get_x.wait()

    def squares(j, _):
        rows = X[pl.ds(pl.multiple_of(j * 128, 128), 128), :].astype(F32)
        SQ[mp, pl.ds(j, 1), :] = to_row(jnp.sum(rows * rows, axis=1, keepdims=True))
        return 0

    lax.fori_loop(0, 8, squares, 0)
    for k in range(1, 8):
        send(SQ.at[mp], SQ.at[mp], sqs.at[k], sqr.at[k], to_mp(k))

    get_picked.wait()
    get_gain.wait()
    live = lax.broadcasted_iota(jnp.int32, (1, 1024), 1) < count[0]
    wanted = jnp.where(live, picked[...], -1)

    def selected(j, _):
        number = lax.broadcasted_iota(jnp.int32, (128, 1024), 0) + j * 128
        hit = jnp.where(wanted == number, 1.0, 0.0)
        inv_c[pl.ds(pl.multiple_of(j * 128, 128), 128), :] = jnp.sum(hit, axis=1, keepdims=True)
        return 0

    lax.fori_loop(0, 8, selected, 0)

    for i, (j, k) in enumerate(near):
        w_arrived(i, (0, j, 0))
    w_cross(14, pl.ds(1, 3), 0)
    w_relay(10, 0, 0)

    for k in range(1, 8):
        arrived(SQ.at[rem(mp + 8 - k, 8)], sqs.at[k], sqr.at[k], to_mp(8 - k))
    total = SQ[0]
    for k in range(1, 8):
        total = total + SQ[k]
    SQ[8] = lax.rsqrt(total / D + EPS)

    def hidden(j, _):
        rows = pl.ds(pl.multiple_of(j * 128, 128), 128)
        inverse = to_col(SQ[8, pl.ds(j, 1), :]) * inv_c[rows, :]
        inv_c[rows, :] = inverse
        normed = X[rows, :].astype(F32) * inverse
        H[rows, :] = (normed * gain[...]).astype(BF16)
        return 0

    arrived(half(block(3), 0), ys.at[1], yr.at[1], to_y(3))
    send(half(block(3), 0), half(block(3), 0), ys.at[5], yr.at[5], to_y(1))
    arrived(half(block(1), 1), ys.at[3], yr.at[3], to_y(1))
    send(half(block(1), 1), half(block(1), 1), ys.at[6], yr.at[6], to_y(3))
    lax.fori_loop(0, 8, hidden, 0)
    arrived(half(block(3), 1), ys.at[2], yr.at[2], to_y(3))
    send(GT.at[block(3)], GT.at[block(3)], ys.at[7], yr.at[7], sibling)
    arrived(half(block(1), 0), ys.at[4], yr.at[4], to_y(1))
    send(GT.at[block(1)], GT.at[block(1)], ys.at[8], yr.at[8], sibling)

    for m in (1, 3, 2):
        w_arrived(2 + m, (0, 0, m))
    for i, (j, k) in enumerate(near):
        w_send(6 + i, (0, 0, later), (0, j, later), to_z(k))
    w_cross(18, 0, later)
    w_relay(14, pl.ds(1, 3), 0)
    arrived(half(block(2), 0), ys.at[5], yr.at[5], to_y(3))
    arrived(half(block(2), 1), ys.at[6], yr.at[6], to_y(1))
    send(GT.at[block(2)], GT.at[block(2)], ys.at[9], yr.at[9], sibling)
    arrived(GT.at[block(0, True)], ys.at[0], yr.at[0], sibling)
    arrived(GT.at[block(3, True)], ys.at[7], yr.at[7], sibling)
    arrived(GT.at[block(1, True)], ys.at[8], yr.at[8], sibling)
    arrived(GT.at[block(2, True)], ys.at[9], yr.at[9], sibling)

    def x_send(i, p, src, dst, d):
        send(src.at[p], dst.at[p], xs.at[i, p, d], xr.at[i, p, d], to_x(1 if d == 0 else 3))

    def x_arrived(i, p, dst, d):
        arrived(dst.at[p], xs.at[i, p, d], xr.at[i, p, d], to_x(3 if d == 0 else 1))

    def terms(p):
        def product(k):
            b = rem(x + k, NX)
            lhs = GT[pl.ds(2 * b, 2)].reshape(256, 1024)
            out = dot(lhs, H[:, 256 * p : 256 * p + 256])
            return out[:, :128].reshape(16, 16, 128), out[:, 128:].reshape(16, 16, 128)

        left, right = product(2)
        S2[p, 0] = left.astype(BF16)
        S2[p, 1] = right.astype(BF16)
        send(S2.at[p, 0], RA.at[p], xs.at[0, p, 0], xr.at[0, p, 0], to_x(1))
        send(S2.at[p, 1], RB.at[p], xs.at[0, p, 1], xr.at[0, p, 1], to_x(3))
        left, right = product(1)
        F1[p] = left
        D1[p] = right.astype(BF16)
        x_send(1, p, D1, DB, 0)
        left, right = product(3)
        D3[p] = left.astype(BF16)
        F3[p] = right
        x_send(1, p, D3, DA, 1)
        left, right = product(0)
        R[p, :, :, :, :128] = left.reshape(4, 4, 16, 128)
        R[p, :, :, :, 128:] = right.reshape(4, 4, 16, 128)

    def relay(p):
        x_arrived(0, p, RA, 0)
        U1[p] = (F1[p] + RA[p].astype(F32)).astype(BF16)
        x_send(2, p, U1, SA, 0)
        x_arrived(0, p, RB, 1)
        U3[p] = (F3[p] + RB[p].astype(F32)).astype(BF16)
        x_send(2, p, U3, SB, 1)

    ways = ((1, 15), (15, 1), (2, 14))

    def owned(p):
        x_arrived(1, p, DB, 0)
        x_arrived(1, p, DA, 1)
        x_arrived(2, p, SA, 0)
        x_arrived(2, p, SB, 1)
        for cols, first, second in ((slice(0, 128), DA, SA), (slice(128, 256), DB, SB)):
            more = first[p].astype(F32) + second[p].astype(F32)
            R[p, :, :, :, cols] = R[p, :, :, :, cols] + more.reshape(4, 4, 16, 128)
        for i, (k, _) in enumerate(ways):
            QA[p, i] = R[p, :, rem(z + k, 4)].astype(BF16)
            send(QA.at[p, i], QR.at[p, i], qs.at[p, i], qr.at[p, i], to_z(k))

    def fourth(p):
        sums = R[p, :, rem(z, 4)]
        for i, (_, k) in enumerate(ways):
            arrived(QR.at[p, i], qs.at[p, i], qr.at[p, i], to_z(k))
            sums = sums + QR[p, i].astype(F32)
        T[p] = sums
        for m in (1, 3, 2):
            mine = T.at[p, rem(lax.div(z, 4) + m, 4)]
            send(mine, TR.at[p, m - 1], ts.at[p, m - 1], tr.at[p, m - 1], to_z(4 * m))

    def complete(p):
        sums = T[p, lax.div(z, 4)]
        for m in (1, 2, 3):
            arrived(TR.at[p, m - 1], ts.at[p, m - 1], tr.at[p, m - 1], to_z(16 - 4 * m))
            sums = sums + TR[p, m - 1]
        wg_out[:, 256 * p : 256 * p + 256] = sums

    def unflip(r, _):
        rows = pl.ds(pl.multiple_of(r * 256, 256), 256)
        G[rows, :] = GT[:, :, rows].reshape(1024, 256).T
        return 0

    def backward(r):
        rows = pl.ds(256 * r, 256)

        def tile(n, _):
            here = pl.ds(pl.multiple_of(n * 256, 256), 256)
            GH[rows, here] = dot(G[rows, :], W[:, :, here].reshape(1024, 256))
            return 0

        lax.fori_loop(0, 4, tile, 0)
        for i in (0, 1):
            j = 2 * r + i
            part = pl.ds(128 * j, 128)
            normed = X[part, :].astype(F32) * inv_c[part, :]
            product = GH[part, :] * normed
            sums = jnp.sum(product, axis=0, keepdims=True)
            for b in range(8):
                piece = sums[:, 128 * b : 128 * b + 128]
                if j == 0:
                    GX[x, b : b + 1, :] = piece
                else:
                    GX[x, b : b + 1, :] = GX[x, b : b + 1, :] + piece
            inner = jnp.sum(gain[...] * product, axis=1, keepdims=True)
            IN[mp, j : j + 1, :] = to_row(inner)

    def w_place(i, j, m):
        there = rem(x + i, NX) * NZ + rem(z + NZ + (0, 1, 2, -1)[j] + 4 * m, NZ)
        W[there] = WR[i, j, m]

    terms(0)
    terms(1)
    for i, (j, k) in enumerate(near):
        w_arrived(6 + i, (0, j, later))
        w_cross(22 + 4 * i, j, later)
    w_relay(18, 0, later)
    terms(2)
    relay(0)
    terms(3)
    relay(1)
    lax.fori_loop(0, 4, unflip, 0)
    owned(0)
    relay(2)
    for i, (j, k) in enumerate(near):
        w_relay(22 + 4 * i, j, later)
    owned(1)
    fourth(0)
    relay(3)
    for j in range(4):
        for m in range(4):
            w_place(0, j, m)
            if j == 0 or m == 0:
                w_place(1, j, m)
                w_place(3, j, m)
    w_relayed(10, 0, 0)
    w_relayed(14, pl.ds(1, 3), 0)
    w_relayed(18, 0, later)
    for i, (j, k) in enumerate(near):
        w_relayed(22 + 4 * i, j, later)
    for j in range(4):
        for m in range(4):
            w_place(2, j, m)
            if j != 0 and m != 0:
                w_place(1, j, m)
                w_place(3, j, m)
    backward(0)
    owned(2)
    fourth(1)
    backward(1)
    owned(3)
    fourth(2)
    backward(2)
    fourth(3)
    backward(3)
    for k in range(1, 8):
        send(IN.at[mp], IN.at[mp], ins.at[k], inr.at[k], to_mp(k))
    for k in range(1, NX):
        send(GX.at[x], GX.at[x], gxs.at[k], gxr.at[k], to_x(k))
    complete(0)
    complete(1)

    def column(r, i):
        return to_col(picked[:, 256 * r + 128 * i : 256 * r + 128 * i + 128].astype(F32))

    def choose(r):
        ids = jnp.concatenate([column(r, 0), column(r, 1)], axis=0).astype(jnp.int32)
        slot = lax.broadcasted_iota(jnp.int32, (256, 1), 0) + 256 * r
        ids = jnp.where(slot < count[0], ids, -1)
        number = lax.broadcasted_iota(jnp.int32, (256, 1024), 1)
        H[pl.ds(256 * r, 256), :] = jnp.where(ids == number, 1.0, 0.0).astype(BF16)

    for r in range(4):
        choose(r)
    for k in range(1, NX):
        arrived(GX.at[rem(x + NX - k, NX)], gxs.at[k], gxr.at[k], to_x(NX - k))
    GZ[z] = GX[0] + GX[1] + GX[2] + GX[3]
    for k in range(1, NZ):
        send(GZ.at[z], GZ.at[z], gzs.at[k], gzr.at[k], to_z(k))
    for k in range(1, 8):
        arrived(IN.at[rem(mp + 8 - k, 8)], ins.at[k], inr.at[k], to_mp(8 - k))
    total = IN[0]
    for k in range(1, 8):
        total = total + IN[k]
    IN[8] = total / D

    def finish(j, _):
        rows = pl.ds(pl.multiple_of(j * 128, 128), 128)
        inner = to_col(IN[8, pl.ds(j, 1), :])
        inverse = inv_c[rows, :]
        normed = X[rows, :].astype(F32) * inverse
        RG[rows, :] = (inverse * (gain[...] * GH[rows, :] - normed * inner)).astype(BF16)
        return 0

    lax.fori_loop(0, 8, finish, 0)

    def place(r):
        rows = pl.ds(256 * r, 256)

        def tile(n, _):
            here = pl.ds(pl.multiple_of(n * 256, 256), 256)
            OUT[rows, here] = dot(H[rows, :], RG[:, here]).astype(BF16)
            return 0

        lax.fori_loop(0, 4, tile, 0)
        copy = pltpu.make_async_copy(OUT.at[rows], rows_out.at[rows], osem.at[r])
        copy.start()
        return copy

    written = [place(r) for r in range(4)]
    complete(2)
    complete(3)
    for k in range(1, NZ):
        arrived(GZ.at[rem(z + NZ - k, NZ)], gzs.at[k], gzr.at[k], to_z(NZ - k))
    total = GZ[0]
    for k in range(1, NZ):
        total = total + GZ[k]
    gg_out[...] = total
    for copy in written:
        copy.wait()
    for copy in pending:
        copy.wait_send()


def deliver(rows_in, wg_in, gg_in, rows_out, wg_out, gg_out, sem):
    copies = [
        pltpu.make_async_copy(wg_in, wg_out, sem.at[8]),
        pltpu.make_async_copy(gg_in, gg_out, sem.at[9]),
    ]
    for i in range(8):
        part = pl.ds(128 * i, 128)
        copies.append(pltpu.make_async_copy(rows_in.at[part], rows_out.at[part], sem.at[i]))
    for copy in copies:
        copy.start()
    for copy in copies:
        copy.wait()


def shards(checkpoint, key_grads, key_weight, norm_gain, picked_rows, row_counts):
    any_space = pl.BlockSpec(memory_space=pl.ANY)
    vmem = pl.BlockSpec(memory_space=pltpu.VMEM)
    smem = pl.BlockSpec(memory_space=pltpu.SMEM)
    dma = pltpu.SemaphoreType.DMA
    piece = (4, 16, 16, 128)
    scratch = [
        pltpu.VMEM((1024, 1024), BF16),
        pltpu.VMEM((1024, 128), BF16),
        pltpu.VMEM((8, 128, 1024), BF16),
        pltpu.VMEM((1024, 1024), BF16),
        pltpu.VMEM((NX, 4, 4, 16, 1024), BF16),
        pltpu.VMEM((NX * NZ, 16, 1024), BF16),
        pltpu.VMEM((1024, 1024), BF16),
        pltpu.VMEM((1024, 1024), F32),
        pltpu.VMEM((1024, 1024), BF16),
        pltpu.VMEM((1024, 1024), BF16),
        pltpu.VMEM((1, 1024), F32),
        pltpu.VMEM((1, 1024), jnp.int32),
        pltpu.VMEM((1024, 1), F32),
        pltpu.VMEM((9, 8, 128), F32),
        pltpu.VMEM((9, 8, 128), F32),
        pltpu.VMEM((NX, 8, 128), F32),
        pltpu.VMEM((NZ, 8, 128), F32),
        pltpu.VMEM((4, 2, 16, 16, 128), BF16),
        pltpu.VMEM(piece, BF16),
        pltpu.VMEM(piece, BF16),
        pltpu.VMEM(piece, F32),
        pltpu.VMEM(piece, F32),
        pltpu.VMEM(piece, BF16),
        pltpu.VMEM(piece, BF16),
        pltpu.VMEM((4, 4, 4, 16, 256), F32),
        *[pltpu.VMEM(piece, BF16) for _ in range(6)],
        pltpu.VMEM((4, 3, 4, 16, 256), BF16),
        pltpu.VMEM((4, 3, 4, 16, 256), BF16),
        pltpu.VMEM((4, 4, 16, 256), F32),
        pltpu.VMEM((4, 3, 16, 256), F32),
        dma((5,)), dma((4,)),
        dma((34,)), dma((34,)),
        dma((10,)), dma((10,)),
        dma((8,)), dma((8,)),
        dma((8,)), dma((8,)),
        dma((NX,)), dma((NX,)),
        dma((NZ,)), dma((NZ,)),
        dma((3, 4, 2)), dma((3, 4, 2)),
        dma((4, 3)), dma((4, 3)),
        dma((4, 3)), dma((4, 3)),
    ]
    row_grads, weight_grad, gain_grad = pl.pallas_call(
        kernel,
        out_shape=(
            jax.ShapeDtypeStruct((1024, 1024), BF16),
            jax.ShapeDtypeStruct((16, 1024), F32),
            jax.ShapeDtypeStruct((8, 128), F32),
        ),
        in_specs=[any_space] * 5 + [smem],
        out_specs=(any_space, vmem, vmem),
        scratch_shapes=scratch,
        compiler_params=pltpu.CompilerParams(
            collective_id=0, has_side_effects=True, vmem_limit_bytes=60 * 1024 * 1024
        ),
        cost_estimate=pl.CostEstimate(flops=6 * 1024**3, bytes_accessed=8 * 1024**2, transcendentals=1024),
        name="norm_key_backward",
    )(checkpoint, key_grads, key_weight, norm_gain.reshape(1, 1024), picked_rows, row_counts)
    row_grads, weight_grad, gain_grad = pl.pallas_call(
        deliver,
        out_shape=(
            jax.ShapeDtypeStruct((1024, 1024), BF16),
            jax.ShapeDtypeStruct((16, 1024), F32),
            jax.ShapeDtypeStruct((8, 128), F32),
        ),
        in_specs=[any_space] * 3,
        out_specs=(any_space,) * 3,
        scratch_shapes=[dma((10,))],
        name="deliver",
    )(row_grads, weight_grad, gain_grad)
    return row_grads, weight_grad, gain_grad.reshape(1024)


def solution(mesh):
    in_specs = (P("dp", "mp"), P("dp", "mp"), P("dp", "mp"), P("mp"), P("dp", None), P("dp"))
    out_specs = (P("dp", "mp"), P("dp", "mp"), P("mp"))
    return jax.shard_map(shards, mesh=mesh, in_specs=in_specs, out_specs=out_specs, check_vma=False)
```

```python
import functools

import jax
import jax.numpy as jnp
from jax import lax
from jax.experimental import pallas as pl
from jax.experimental.pallas import tpu as pltpu
from jax.sharding import PartitionSpec as P

D = 8192
EPS = 1e-05
NX, NZ, NY = 4, 16, 4
MESH = pl.DeviceIdType.MESH
F32, BF16 = jnp.float32, jnp.bfloat16


def rem(a, n):
    return lax.rem(a, n)


def dot(a, b):
    return jnp.dot(a, b, preferred_element_type=F32)


def kernel(
    x_in, kg_in, w_in, gain_in, picked_in, count_in,
    rows_out, wg_out, gg_out,
    X, KG, GT, G, WR, W, H, GH, RG, OUT,
    gain, picked, count, inv_c,
    SQ, IN, GX, GZ,
    S2, D1, D3, F1, F3, V, U1, U3, R,
    RA, RB, DA, DB, SA, SB, QA, QR, T, TR,
    lsem, osem, ws, wr, ys, yr, sqs, sqr, ins, inr, gxs, gxr, gzs, gzr,
    xs, xr, qs, qr, ts, tr,
):
    dp, mp = lax.axis_index("dp"), lax.axis_index("mp")
    x, z = lax.div(dp, NZ), rem(dp, NZ)
    y, c = lax.div(mp, 2), rem(mp, 2)
    pending = []

    def to_x(k):
        return (rem(x + k, NX) * NZ + z, mp)

    def to_z(k):
        return (x * NZ + rem(z + k, NZ), mp)

    def to_y(k):
        return (dp, rem(y + k, NY) * 2 + c)

    def to_mp(k):
        return (dp, rem(mp + k, 8))

    sibling = (dp, 2 * y + 1 - c)

    def send(src, dst, ss, rs, dev):
        copy = pltpu.make_async_remote_copy(
            src_ref=src, dst_ref=dst, send_sem=ss, recv_sem=rs, device_id=dev, device_id_type=MESH
        )
        copy.start()
        pending.append(copy)

    def arrived(dst, ss, rs, dev):
        pltpu.make_async_remote_copy(
            src_ref=dst, dst_ref=dst, send_sem=ss, recv_sem=rs, device_id=dev, device_id_type=MESH
        ).wait_recv()

    get_kg = pltpu.make_async_copy(kg_in, KG, lsem.at[0])
    get_x = pltpu.make_async_copy(x_in, X, lsem.at[1])
    get_w = pltpu.make_async_copy(w_in, WR.at[0, 0, 0], lsem.at[2])
    get_gain = pltpu.make_async_copy(gain_in, gain, lsem.at[3])
    get_picked = pltpu.make_async_copy(picked_in, picked, lsem.at[4])
    get_count = pltpu.make_async_copy(count_in, count, lsem.at[5])
    get_kg.start()
    get_w.start()
    get_x.start()
    get_gain.start()
    get_picked.start()
    get_count.start()

    barrier = pltpu.get_barrier_semaphore()
    for k in range(1, NZ):
        pl.semaphore_signal(barrier, inc=1, device_id=to_z(k), device_id_type=MESH)
    for k in range(1, NX):
        pl.semaphore_signal(barrier, inc=1, device_id=to_x(k), device_id_type=MESH)
    for k in range(1, 8):
        pl.semaphore_signal(barrier, inc=1, device_id=to_mp(k), device_id_type=MESH)

    get_kg.wait()

    def flip(j, _):
        rows = pl.ds(pl.multiple_of(j * 128, 128), 128)
        GT[mp, :, rows] = KG[rows, :].T
        return 0

    lax.fori_loop(0, 8, flip, 0)
    get_w.wait()
    pl.semaphore_wait(barrier, 7 + NX - 1 + NZ - 1)

    whole, most, rest = pl.ds(0, 1024), pl.ds(0, 512), pl.ds(512, 512)
    later = pl.ds(1, 3)

    def w_send(i, src, dst, dev, cols=whole):
        send(WR.at[(*src, slice(None), cols)], WR.at[(*dst, slice(None), cols)], ws.at[i], wr.at[i], dev)

    def w_arrived(i, dst, cols=whole):
        arrived(WR.at[(*dst, slice(None), cols)], ws.at[i], wr.at[i], to_x(1))

    near = ((1, 15), (3, 1), (2, 14))

    def w_cross(i, j, m, cols=whole):
        w_send(i, (0, j, m), (1, j, m), to_x(3), cols)
        w_send(i + 1, (0, j, m), (3, j, m), to_x(1), cols)

    def halves(cols):
        size = cols.size // 2
        return pl.ds(0, size), pl.ds(size, size)

    def w_relay(i, j, m, cols=whole):
        low, high = halves(cols)
        w_arrived(i, (1, j, m), cols)
        w_send(i + 2, (1, j, m), (2, j, m), to_x(3), low)
        w_arrived(i + 1, (3, j, m), cols)
        w_send(i + 3, (3, j, m), (2, j, m), to_x(1), high)

    def w_relayed(i, j, m, cols=whole):
        low, high = halves(cols)
        w_arrived(i + 2, (2, j, m), low)
        w_arrived(i + 3, (2, j, m), high)

    for i, (j, k) in enumerate(near):
        w_send(i, (0, 0, 0), (0, j, 0), to_z(k))
    w_cross(10, 0, 0)
    for m in (1, 3, 2):
        w_send(2 + m, (0, 0, 0), (0, 0, m), to_z(16 - 4 * m))

    def block(k, other=False):
        return rem(y + k, NY) * 2 + ((1 - c) if other else c)

    def half(b, h):
        return GT.at[b, pl.ds(64 * h, 64), :]

    send(half(mp, 0), half(mp, 0), ys.at[1], yr.at[1], to_y(1))
    send(half(mp, 1), half(mp, 1), ys.at[3], yr.at[3], to_y(3))
    send(half(mp, 1), half(mp, 1), ys.at[2], yr.at[2], to_y(1))
    send(half(mp, 0), half(mp, 0), ys.at[4], yr.at[4], to_y(3))
    send(GT.at[mp], GT.at[mp], ys.at[0], yr.at[0], sibling)

    eye = lax.broadcasted_iota(jnp.int32, (128, 128), 0) == lax.broadcasted_iota(
        jnp.int32, (128, 128), 1
    )

    def to_row(col):
        return jnp.sum(jnp.where(eye, col, 0.0), axis=0, keepdims=True)

    def to_col(row):
        return jnp.sum(jnp.where(eye, row, 0.0), axis=1, keepdims=True)

    get_x.wait()

    def squares(j, _):
        rows = X[pl.ds(pl.multiple_of(j * 128, 128), 128), :].astype(F32)
        SQ[mp, pl.ds(j, 1), :] = to_row(jnp.sum(rows * rows, axis=1, keepdims=True))
        return 0

    lax.fori_loop(0, 8, squares, 0)
    for k in range(1, 8):
        send(SQ.at[mp], SQ.at[mp], sqs.at[k], sqr.at[k], to_mp(k))

    get_picked.wait()
    get_count.wait()
    get_gain.wait()
    live = lax.broadcasted_iota(jnp.int32, (1, 1024), 1) < count[0]
    wanted = jnp.where(live, picked[...], -1)

    def selected(j, _):
        number = lax.broadcasted_iota(jnp.int32, (128, 1024), 0) + j * 128
        hit = jnp.where(wanted == number, 1.0, 0.0)
        inv_c[pl.ds(pl.multiple_of(j * 128, 128), 128), :] = jnp.sum(hit, axis=1, keepdims=True)
        return 0

    lax.fori_loop(0, 8, selected, 0)

    for i, (j, k) in enumerate(near):
        w_arrived(i, (0, j, 0))
    w_cross(14, pl.ds(1, 3), 0)
    w_relay(10, 0, 0)

    arrived(half(block(3), 0), ys.at[1], yr.at[1], to_y(3))
    send(half(block(3), 0), half(block(3), 0), ys.at[5], yr.at[5], to_y(1))
    arrived(half(block(1), 1), ys.at[3], yr.at[3], to_y(1))
    send(half(block(1), 1), half(block(1), 1), ys.at[6], yr.at[6], to_y(3))
    for k in range(1, 8):
        arrived(SQ.at[rem(mp + 8 - k, 8)], sqs.at[k], sqr.at[k], to_mp(8 - k))
    total = SQ[0]
    for k in range(1, 8):
        total = total + SQ[k]
    SQ[8] = lax.rsqrt(total / D + EPS)

    def hidden(j, _):
        rows = pl.ds(pl.multiple_of(j * 128, 128), 128)
        inverse = to_col(SQ[8, pl.ds(j, 1), :]) * inv_c[rows, :]
        inv_c[rows, :] = inverse
        normed = X[rows, :].astype(F32) * inverse
        H[rows, :] = (normed * gain[...]).astype(BF16)
        return 0

    lax.fori_loop(0, 8, hidden, 0)
    arrived(half(block(3), 1), ys.at[2], yr.at[2], to_y(3))
    send(GT.at[block(3)], GT.at[block(3)], ys.at[7], yr.at[7], sibling)
    arrived(half(block(1), 0), ys.at[4], yr.at[4], to_y(1))
    send(GT.at[block(1)], GT.at[block(1)], ys.at[8], yr.at[8], sibling)

    for m in (1, 3, 2):
        w_arrived(2 + m, (0, 0, m))
    for i, (j, k) in enumerate(near):
        w_send(6 + i, (0, 0, later), (0, j, later), to_z(k))
    w_cross(18, 0, later)
    w_relay(14, pl.ds(1, 3), 0)
    arrived(half(block(2), 0), ys.at[5], yr.at[5], to_y(3))
    arrived(half(block(2), 1), ys.at[6], yr.at[6], to_y(1))
    send(GT.at[block(2)], GT.at[block(2)], ys.at[9], yr.at[9], sibling)
    arrived(GT.at[block(0, True)], ys.at[0], yr.at[0], sibling)
    arrived(GT.at[block(3, True)], ys.at[7], yr.at[7], sibling)
    arrived(GT.at[block(1, True)], ys.at[8], yr.at[8], sibling)
    arrived(GT.at[block(2, True)], ys.at[9], yr.at[9], sibling)

    def x_send(i, p, src, dst, d):
        send(src.at[p], dst.at[p], xs.at[i, p, d], xr.at[i, p, d], to_x(1 if d == 0 else 3))

    def x_arrived(i, p, dst, d):
        arrived(dst.at[p], xs.at[i, p, d], xr.at[i, p, d], to_x(3 if d == 0 else 1))

    def terms(p):
        def product(k):
            b = rem(x + k, NX)
            lhs = GT[pl.ds(2 * b, 2)].reshape(256, 1024)
            out = dot(lhs, H[:, 256 * p : 256 * p + 256])
            return out[:, :128].reshape(16, 16, 128), out[:, 128:].reshape(16, 16, 128)

        left, right = product(2)
        S2[p, 0] = left.astype(BF16)
        S2[p, 1] = right.astype(BF16)
        send(S2.at[p, 0], RA.at[p], xs.at[0, p, 0], xr.at[0, p, 0], to_x(1))
        send(S2.at[p, 1], RB.at[p], xs.at[0, p, 1], xr.at[0, p, 1], to_x(3))
        left, right = product(1)
        F1[p] = left
        D1[p] = right.astype(BF16)
        left, right = product(3)
        D3[p] = left.astype(BF16)
        F3[p] = right
        left, right = product(0)
        V[p, 0] = left
        V[p, 1] = right
        R[p, :, :, :, :128] = left.reshape(4, 4, 16, 128)
        R[p, :, :, :, 128:] = right.reshape(4, 4, 16, 128)

    def relay(p):
        x_arrived(0, p, RA, 0)
        U1[p] = (F1[p] + RA[p].astype(F32)).astype(BF16)
        x_send(2, p, U1, SA, 0)
        x_send(1, p, D1, DB, 0)
        x_arrived(0, p, RB, 1)
        U3[p] = (F3[p] + RB[p].astype(F32)).astype(BF16)
        x_send(2, p, U3, SB, 1)
        x_send(1, p, D3, DA, 1)

    ways = ((1, 15), (15, 1), (2, 14))

    def owned(p):
        x_arrived(1, p, DB, 0)
        x_arrived(1, p, DA, 1)
        x_arrived(2, p, SA, 0)
        x_arrived(2, p, SB, 1)
        for cols, first, second in ((slice(0, 128), DA, SA), (slice(128, 256), DB, SB)):
            more = first[p].astype(F32) + second[p].astype(F32)
            R[p, :, :, :, cols] = R[p, :, :, :, cols] + more.reshape(4, 4, 16, 128)
        for i, (k, _) in enumerate(ways):
            QA[p, i] = R[p, :, rem(z + k, 4)].astype(BF16)
            send(QA.at[p, i], QR.at[p, i], qs.at[p, i], qr.at[p, i], to_z(k))

    def fourth(p):
        sums = R[p, :, rem(z, 4)]
        for i, (_, k) in enumerate(ways):
            arrived(QR.at[p, i], qs.at[p, i], qr.at[p, i], to_z(k))
            sums = sums + QR[p, i].astype(F32)
        T[p] = sums
        for m in (1, 3, 2):
            mine = T.at[p, rem(lax.div(z, 4) + m, 4)]
            send(mine, TR.at[p, m - 1], ts.at[p, m - 1], tr.at[p, m - 1], to_z(4 * m))

    def complete(p):
        sums = T[p, lax.div(z, 4)]
        for m in (1, 2, 3):
            arrived(TR.at[p, m - 1], ts.at[p, m - 1], tr.at[p, m - 1], to_z(16 - 4 * m))
            sums = sums + TR[p, m - 1]
        wg_out[:, 256 * p : 256 * p + 256] = sums

    def unflip(r, _):
        rows = pl.ds(pl.multiple_of(r * 256, 256), 256)
        G[rows, :] = GT[:, :, rows].reshape(1024, 256).T
        return 0

    def backward(n):
        here = pl.ds(256 * n, 256)
        GH[:, here] = dot(G[...], W[:, :, here].reshape(1024, 256))

    def entered(j):
        part = pl.ds(128 * j, 128)
        normed = X[part, :].astype(F32) * inv_c[part, :]
        inner = jnp.sum(gain[...] * GH[part, :] * normed, axis=1, keepdims=True)
        IN[mp, j : j + 1, :] = to_row(inner)

    def gain_terms(p):
        for h, kept in enumerate(((V.at[p, 0], F1, S2.at[p, 0], D3), (V.at[p, 1], D1, S2.at[p, 1], F3))):
            b = 2 * p + h
            cols = pl.ds(128 * b, 128)
            sums = jnp.zeros((1, 128), F32)
            for k, ref in enumerate(kept):
                term = (ref[p] if k % 2 else ref[...]).astype(F32)
                rows = W[pl.ds(16 * rem(x + k, NX), 16), :, cols].astype(F32)
                sums = sums + jnp.sum((rows * term).reshape(256, 128), axis=0, keepdims=True)
            GX[x, b : b + 1, :] = sums / gain[:, cols]

    def w_place(i, j, m):
        there = rem(x + i, NX) * NZ + rem(z + NZ + (0, 1, 2, -1)[j] + 4 * m, NZ)
        W[there] = WR[i, j, m]

    def column(r, i):
        return to_col(picked[:, 256 * r + 128 * i : 256 * r + 128 * i + 128].astype(F32))

    def choose(r):
        ids = jnp.concatenate([column(r, 0), column(r, 1)], axis=0).astype(jnp.int32)
        slot = lax.broadcasted_iota(jnp.int32, (256, 1), 0) + 256 * r
        ids = jnp.where(slot < count[0], ids, -1)
        number = lax.broadcasted_iota(jnp.int32, (256, 1024), 1)
        H[pl.ds(256 * r, 256), :] = jnp.where(ids == number, 1.0, 0.0).astype(BF16)

    across = pl.ds(1, 3)

    def last_cross(i):
        w_arrived(6 + i, (0, near[i][0], later))
        w_cross(22 + 4 * i, near[i][0], later, most)

    terms(0)
    w_relayed(10, 0, 0)
    terms(1)
    w_relay(18, 0, later)
    w_relayed(14, pl.ds(1, 3), 0)
    terms(2)
    relay(0)
    terms(3)
    w_relayed(18, 0, later)
    for i, (j, k) in enumerate(near):
        w_send(34 + i, (across, 0, later), (across, j, later), to_z(k), rest)
    relay(1)
    last_cross(0)
    relay(2)
    last_cross(1)
    lax.fori_loop(0, 4, unflip, 0)
    owned(0)
    relay(3)
    last_cross(2)
    for j in range(4):
        for m in range(4):
            w_place(0, j, m)
            if j == 0 or m == 0:
                for i in (1, 2, 3):
                    w_place(i, j, m)
    owned(1)
    fourth(0)
    w_relay(22, near[0][0], later, most)
    for r in range(4):
        choose(r)
    owned(2)
    fourth(1)
    w_relay(26, near[1][0], later, most)
    w_relay(30, near[2][0], later, most)
    for i, (j, k) in enumerate(near):
        w_arrived(34 + i, (across, j, later), rest)
    owned(3)
    for i, (j, k) in enumerate(near):
        w_relayed(22 + 4 * i, j, later, most)
    for j in (1, 2, 3):
        for m in (1, 2, 3):
            for i in (1, 2, 3):
                w_place(i, j, m)
    for p in range(4):
        gain_terms(p)
    for k in range(1, NX):
        send(GX.at[x], GX.at[x], gxs.at[k], gxr.at[k], to_x(k))
    fourth(2)
    backward(0)
    backward(1)
    fourth(3)
    backward(2)
    backward(3)
    for j in range(8):
        entered(j)
    for k in range(1, 8):
        send(IN.at[mp], IN.at[mp], ins.at[k], inr.at[k], to_mp(k))
    for k in range(1, NX):
        arrived(GX.at[rem(x + NX - k, NX)], gxs.at[k], gxr.at[k], to_x(NX - k))
    GZ[z] = GX[0] + GX[1] + GX[2] + GX[3]
    for k in range(1, NZ):
        send(GZ.at[z], GZ.at[z], gzs.at[k], gzr.at[k], to_z(k))
    complete(0)
    complete(1)
    for k in range(1, 8):
        arrived(IN.at[rem(mp + 8 - k, 8)], ins.at[k], inr.at[k], to_mp(8 - k))
    total = IN[0]
    for k in range(1, 8):
        total = total + IN[k]
    IN[8] = total / D

    def finish(j, _):
        rows = pl.ds(pl.multiple_of(j * 128, 128), 128)
        inner = to_col(IN[8, pl.ds(j, 1), :])
        inverse = inv_c[rows, :]
        normed = X[rows, :].astype(F32) * inverse
        RG[rows, :] = (inverse * (gain[...] * GH[rows, :] - normed * inner)).astype(BF16)
        return 0

    lax.fori_loop(0, 8, finish, 0)

    def place(n):
        here = pl.ds(256 * n, 256)
        OUT[:, here] = dot(H[...], RG[:, here]).astype(BF16)
        copy = pltpu.make_async_copy(OUT.at[:, here], rows_out.at[:, here], osem.at[n])
        copy.start()
        return copy

    written = [place(r) for r in range(4)]
    complete(2)
    complete(3)
    for k in range(1, NZ):
        arrived(GZ.at[rem(z + NZ - k, NZ)], gzs.at[k], gzr.at[k], to_z(NZ - k))
    total = GZ[0]
    for k in range(1, NZ):
        total = total + GZ[k]
    gg_out[...] = total
    for copy in written:
        copy.wait()
    for copy in pending:
        copy.wait_send()


def deliver(rows_in, wg_in, gg_in, rows_out, wg_out, gg_out, rows, wg, gg, sem):
    def move(i, src, by, dst):
        return (
            pltpu.make_async_copy(src, by, sem.at[0, i]),
            pltpu.make_async_copy(by, dst, sem.at[1, i]),
        )

    moves = [
        move(i, *(ref.at[pl.ds(128 * i, 128)] for ref in (rows_in, rows, rows_out))) for i in range(8)
    ]
    moves += [move(8, wg_in, wg, wg_out), move(9, gg_in, gg, gg_out)]
    for first, _ in moves:
        first.start()
    for first, second in moves:
        first.wait()
        second.start()
    for _, second in moves:
        second.wait()


def shards(checkpoint, key_grads, key_weight, norm_gain, picked_rows, row_counts):
    any_space = pl.BlockSpec(memory_space=pl.ANY)
    vmem = pl.BlockSpec(memory_space=pltpu.VMEM)
    dma = pltpu.SemaphoreType.DMA
    piece = (4, 16, 16, 128)
    scratch = [
        pltpu.VMEM((1024, 1024), BF16),
        pltpu.VMEM((1024, 128), BF16),
        pltpu.VMEM((8, 128, 1024), BF16),
        pltpu.VMEM((1024, 1024), BF16),
        pltpu.VMEM((NX, 4, 4, 16, 1024), BF16),
        pltpu.VMEM((NX * NZ, 16, 1024), BF16),
        pltpu.VMEM((1024, 1024), BF16),
        pltpu.VMEM((1024, 1024), F32),
        pltpu.VMEM((1024, 1024), BF16),
        pltpu.VMEM((1024, 1024), BF16),
        pltpu.VMEM((1, 1024), F32),
        pltpu.VMEM((1, 1024), jnp.int32),
        pltpu.SMEM((1,), jnp.int32),
        pltpu.VMEM((1024, 1), F32),
        pltpu.VMEM((9, 8, 128), F32),
        pltpu.VMEM((9, 8, 128), F32),
        pltpu.VMEM((NX, 8, 128), F32),
        pltpu.VMEM((NZ, 8, 128), F32),
        pltpu.VMEM((4, 2, 16, 16, 128), BF16),
        pltpu.VMEM(piece, BF16),
        pltpu.VMEM(piece, BF16),
        pltpu.VMEM(piece, F32),
        pltpu.VMEM(piece, F32),
        pltpu.VMEM((4, 2, 16, 16, 128), F32),
        pltpu.VMEM(piece, BF16),
        pltpu.VMEM(piece, BF16),
        pltpu.VMEM((4, 4, 4, 16, 256), F32),
        *[pltpu.VMEM(piece, BF16) for _ in range(6)],
        pltpu.VMEM((4, 3, 4, 16, 256), BF16),
        pltpu.VMEM((4, 3, 4, 16, 256), BF16),
        pltpu.VMEM((4, 4, 16, 256), F32),
        pltpu.VMEM((4, 3, 16, 256), F32),
        dma((6,)), dma((4,)),
        dma((37,)), dma((37,)),
        dma((10,)), dma((10,)),
        dma((8,)), dma((8,)),
        dma((8,)), dma((8,)),
        dma((NX,)), dma((NX,)),
        dma((NZ,)), dma((NZ,)),
        dma((3, 4, 2)), dma((3, 4, 2)),
        dma((4, 3)), dma((4, 3)),
        dma((4, 3)), dma((4, 3)),
    ]
    row_grads, weight_grad, gain_grad = pl.pallas_call(
        kernel,
        out_shape=(
            jax.ShapeDtypeStruct((1024, 1024), BF16),
            jax.ShapeDtypeStruct((16, 1024), F32),
            jax.ShapeDtypeStruct((8, 128), F32),
        ),
        in_specs=[any_space] * 6,
        out_specs=(any_space, vmem, vmem),
        scratch_shapes=scratch,
        compiler_params=pltpu.CompilerParams(
            collective_id=0, has_side_effects=True, vmem_limit_bytes=60 * 1024 * 1024
        ),
        cost_estimate=pl.CostEstimate(flops=6 * 1024**3, bytes_accessed=8 * 1024**2, transcendentals=1024),
        name="norm_key_backward",
    )(checkpoint, key_grads, key_weight, norm_gain.reshape(1, 1024), picked_rows, row_counts)
    row_grads, weight_grad, gain_grad = pl.pallas_call(
        deliver,
        out_shape=(
            jax.ShapeDtypeStruct((1024, 1024), BF16),
            jax.ShapeDtypeStruct((16, 1024), F32),
            jax.ShapeDtypeStruct((8, 128), F32),
        ),
        in_specs=[any_space] * 3,
        out_specs=(any_space,) * 3,
        scratch_shapes=[
            pltpu.VMEM((1024, 1024), BF16),
            pltpu.VMEM((16, 1024), F32),
            pltpu.VMEM((8, 128), F32),
            dma((2, 10)),
        ],
        compiler_params=pltpu.CompilerParams(vmem_limit_bytes=60 * 1024 * 1024),
        name="deliver",
    )(row_grads, weight_grad, gain_grad)
    return row_grads, weight_grad, gain_grad.reshape(1024)


def solution(mesh):
    in_specs = (P("dp", "mp"), P("dp", "mp"), P("dp", "mp"), P("mp"), P("dp", None), P("dp"))
    out_specs = (P("dp", "mp"), P("dp", "mp"), P("mp"))
    return jax.shard_map(shards, mesh=mesh, in_specs=in_specs, out_specs=out_specs, check_vma=False)
```

```python
import functools

import jax
import jax.numpy as jnp
from jax import lax
from jax.experimental import pallas as pl
from jax.experimental.pallas import tpu as pltpu
from jax.sharding import PartitionSpec as P

D = 8192
EPS = 1e-05
NX, NZ, NY = 4, 16, 4
MESH = pl.DeviceIdType.MESH
F32, BF16 = jnp.float32, jnp.bfloat16


def rem(a, n):
    return lax.rem(a, n)


def dot(a, b):
    return jnp.dot(a, b, preferred_element_type=F32)


def kernel(
    x_in, kg_in, w_in, gain_in, picked_in, count_in,
    rows_out, wg_out, gg_out,
    X, KG, GT, G, WR, W, H, GH, RG, OUT,
    gain, picked, count, inv_c,
    SQ, IN, GX, GZ,
    S2, D1, D3, F1, F3, V, U1, U3, R,
    RA, RB, DA, DB, SA, SB, QA, QR, T, TR,
    AZ, QB, QC, Y, ZS, ZR,
    lsem, osem, ws, wr, ys, yr, sqs, sqr, ins, inr, gxs, gxr, gzs, gzr,
    xs, xr, qs, qr, ts, tr, qbs, qbr, zxs, zxr,
):
    dp, mp = lax.axis_index("dp"), lax.axis_index("mp")
    x, z = lax.div(dp, NZ), rem(dp, NZ)
    y, c = lax.div(mp, 2), rem(mp, 2)
    pending = []

    def to_x(k):
        return (rem(x + k, NX) * NZ + z, mp)

    def to_z(k):
        return (x * NZ + rem(z + k, NZ), mp)

    def to_y(k):
        return (dp, rem(y + k, NY) * 2 + c)

    def to_mp(k):
        return (dp, rem(mp + k, 8))

    sibling = (dp, 2 * y + 1 - c)

    def send(src, dst, ss, rs, dev):
        copy = pltpu.make_async_remote_copy(
            src_ref=src, dst_ref=dst, send_sem=ss, recv_sem=rs, device_id=dev, device_id_type=MESH
        )
        copy.start()
        pending.append(copy)

    def arrived(dst, ss, rs, dev):
        pltpu.make_async_remote_copy(
            src_ref=dst, dst_ref=dst, send_sem=ss, recv_sem=rs, device_id=dev, device_id_type=MESH
        ).wait_recv()

    def wait_sends():
        while pending:
            pending.pop().wait_send()

    get_kg = pltpu.make_async_copy(kg_in, KG, lsem.at[0])
    get_x = pltpu.make_async_copy(x_in, X, lsem.at[1])
    get_w = pltpu.make_async_copy(w_in, WR.at[0, 0, 0], lsem.at[2])
    get_gain = pltpu.make_async_copy(gain_in, gain, lsem.at[3])
    get_picked = pltpu.make_async_copy(picked_in, picked, lsem.at[4])
    get_count = pltpu.make_async_copy(count_in, count, lsem.at[5])
    get_kg.start()
    get_w.start()
    get_x.start()
    get_gain.start()
    get_picked.start()
    get_count.start()

    barrier = pltpu.get_barrier_semaphore()
    for k in range(1, NZ):
        pl.semaphore_signal(barrier, inc=1, device_id=to_z(k), device_id_type=MESH)
    for k in range(1, NX):
        pl.semaphore_signal(barrier, inc=1, device_id=to_x(k), device_id_type=MESH)
    for k in range(1, 8):
        pl.semaphore_signal(barrier, inc=1, device_id=to_mp(k), device_id_type=MESH)

    get_kg.wait()

    def flip(j, _):
        rows = pl.ds(pl.multiple_of(j * 128, 128), 128)
        GT[mp, :, rows] = KG[rows, :].T
        return 0

    lax.fori_loop(0, 8, flip, 0)
    get_w.wait()
    pl.semaphore_wait(barrier, 7 + NX - 1 + NZ - 1)

    whole, most, rest = pl.ds(0, 1024), pl.ds(0, 512), pl.ds(512, 512)
    later = pl.ds(1, 3)

    def w_send(i, src, dst, dev, cols=whole):
        send(WR.at[(*src, slice(None), cols)], WR.at[(*dst, slice(None), cols)], ws.at[i], wr.at[i], dev)

    def w_arrived(i, dst, cols=whole):
        arrived(WR.at[(*dst, slice(None), cols)], ws.at[i], wr.at[i], to_x(1))

    near = ((1, 15), (3, 1), (2, 14 - 12 * c))

    def w_cross(i, j, m, cols=whole):
        w_send(i, (0, j, m), (1, j, m), to_x(3), cols)
        w_send(i + 1, (0, j, m), (3, j, m), to_x(1), cols)

    def halves(cols):
        size = cols.size // 2
        return pl.ds(0, size), pl.ds(size, size)

    def w_relay(i, j, m, cols=whole):
        low, high = halves(cols)
        w_arrived(i, (1, j, m), cols)
        w_send(i + 2, (1, j, m), (2, j, m), to_x(3), low)
        w_arrived(i + 1, (3, j, m), cols)
        w_send(i + 3, (3, j, m), (2, j, m), to_x(1), high)

    def w_relayed(i, j, m, cols=whole):
        low, high = halves(cols)
        w_arrived(i + 2, (2, j, m), low)
        w_arrived(i + 3, (2, j, m), high)

    for i, (j, k) in enumerate(near):
        w_send(i, (0, 0, 0), (0, j, 0), to_z(k))
    w_cross(10, 0, 0)
    for m in (2, 1, 3):
        w_send(2 + m, (0, 0, 0), (0, 0, m), to_z(16 - 4 * m))

    def block(k, other=False):
        return rem(y + k, NY) * 2 + ((1 - c) if other else c)

    def half(b, h):
        return GT.at[b, pl.ds(64 * h, 64), :]

    send(half(mp, 0), half(mp, 0), ys.at[1], yr.at[1], to_y(1))
    send(half(mp, 1), half(mp, 1), ys.at[3], yr.at[3], to_y(3))
    send(half(mp, 1), half(mp, 1), ys.at[2], yr.at[2], to_y(1))
    send(half(mp, 0), half(mp, 0), ys.at[4], yr.at[4], to_y(3))
    send(GT.at[mp], GT.at[mp], ys.at[0], yr.at[0], sibling)

    eye = lax.broadcasted_iota(jnp.int32, (128, 128), 0) == lax.broadcasted_iota(
        jnp.int32, (128, 128), 1
    )

    def to_row(col):
        return jnp.sum(jnp.where(eye, col, 0.0), axis=0, keepdims=True)

    def to_col(row):
        return jnp.sum(jnp.where(eye, row, 0.0), axis=1, keepdims=True)

    get_x.wait()

    def squares(j, _):
        rows = X[pl.ds(pl.multiple_of(j * 128, 128), 128), :].astype(F32)
        SQ[mp, pl.ds(j, 1), :] = to_row(jnp.sum(rows * rows, axis=1, keepdims=True))
        return 0

    lax.fori_loop(0, 8, squares, 0)
    for k in range(1, 8):
        send(SQ.at[mp], SQ.at[mp], sqs.at[k], sqr.at[k], to_mp(k))

    get_picked.wait()
    get_count.wait()
    get_gain.wait()
    live = lax.broadcasted_iota(jnp.int32, (1, 1024), 1) < count[0]
    wanted = jnp.where(live, picked[...], -1)

    def selected(j, _):
        number = lax.broadcasted_iota(jnp.int32, (128, 1024), 0) + j * 128
        hit = jnp.where(wanted == number, 1.0, 0.0)
        inv_c[pl.ds(pl.multiple_of(j * 128, 128), 128), :] = jnp.sum(hit, axis=1, keepdims=True)
        return 0

    lax.fori_loop(0, 8, selected, 0)

    for i, (j, k) in enumerate(near):
        w_arrived(i, (0, j, 0))
    w_cross(14, pl.ds(1, 3), 0)
    w_relay(10, 0, 0)

    arrived(half(block(3), 0), ys.at[1], yr.at[1], to_y(3))
    send(half(block(3), 0), half(block(3), 0), ys.at[5], yr.at[5], to_y(1))
    arrived(half(block(1), 1), ys.at[3], yr.at[3], to_y(1))
    send(half(block(1), 1), half(block(1), 1), ys.at[6], yr.at[6], to_y(3))
    for k in range(1, 8):
        arrived(SQ.at[rem(mp + 8 - k, 8)], sqs.at[k], sqr.at[k], to_mp(8 - k))
    total = SQ[0]
    for k in range(1, 8):
        total = total + SQ[k]
    SQ[8] = lax.rsqrt(total / D + EPS)

    def hidden(j, _):
        rows = pl.ds(pl.multiple_of(j * 128, 128), 128)
        inverse = to_col(SQ[8, pl.ds(j, 1), :]) * inv_c[rows, :]
        inv_c[rows, :] = inverse
        normed = X[rows, :].astype(F32) * inverse
        H[rows, :] = (normed * gain[...]).astype(BF16)
        return 0

    lax.fori_loop(0, 8, hidden, 0)
    arrived(half(block(3), 1), ys.at[2], yr.at[2], to_y(3))
    send(GT.at[block(3)], GT.at[block(3)], ys.at[7], yr.at[7], sibling)
    arrived(half(block(1), 0), ys.at[4], yr.at[4], to_y(1))
    send(GT.at[block(1)], GT.at[block(1)], ys.at[8], yr.at[8], sibling)

    for m in (1, 3, 2):
        w_arrived(2 + m, (0, 0, m))
    for i, (j, k) in enumerate(near):
        w_send(6 + i, (0, 0, later), (0, j, later), to_z(k))
    w_cross(18, 0, later)
    w_relay(14, pl.ds(1, 3), 0)
    arrived(half(block(2), 0), ys.at[5], yr.at[5], to_y(3))
    arrived(half(block(2), 1), ys.at[6], yr.at[6], to_y(1))
    send(GT.at[block(2)], GT.at[block(2)], ys.at[9], yr.at[9], sibling)
    arrived(GT.at[block(0, True)], ys.at[0], yr.at[0], sibling)
    arrived(GT.at[block(3, True)], ys.at[7], yr.at[7], sibling)
    arrived(GT.at[block(1, True)], ys.at[8], yr.at[8], sibling)
    arrived(GT.at[block(2, True)], ys.at[9], yr.at[9], sibling)

    def x_send(i, p, src, dst, d):
        send(src.at[p], dst.at[p], xs.at[i, p, d], xr.at[i, p, d], to_x(1 if d == 0 else 3))

    def x_arrived(i, p, dst, d):
        arrived(dst.at[p], xs.at[i, p, d], xr.at[i, p, d], to_x(3 if d == 0 else 1))

    def terms(p):
        def product(k):
            b = rem(x + k, NX)
            lhs = GT[pl.ds(2 * b, 2)].reshape(256, 1024)
            out = dot(lhs, H[:, 256 * p : 256 * p + 256])
            return out[:, :128].reshape(16, 16, 128), out[:, 128:].reshape(16, 16, 128)

        left, right = product(2)
        S2[p, 0] = left.astype(BF16)
        S2[p, 1] = right.astype(BF16)
        send(S2.at[p, 0], RA.at[p], xs.at[0, p, 0], xr.at[0, p, 0], to_x(1))
        send(S2.at[p, 1], RB.at[p], xs.at[0, p, 1], xr.at[0, p, 1], to_x(3))
        left, right = product(1)
        F1[p] = left
        D1[p] = right.astype(BF16)
        left, right = product(3)
        D3[p] = left.astype(BF16)
        F3[p] = right
        left, right = product(0)
        V[p, 0] = left
        V[p, 1] = right
        R[p, :, :, :, :128] = left.reshape(4, 4, 16, 128)
        R[p, :, :, :, 128:] = right.reshape(4, 4, 16, 128)

    def relay(p):
        x_arrived(0, p, RA, 0)
        U1[p] = (F1[p] + RA[p].astype(F32)).astype(BF16)
        x_send(2, p, U1, SA, 0)
        x_send(1, p, D1, DB, 0)
        x_arrived(0, p, RB, 1)
        U3[p] = (F3[p] + RB[p].astype(F32)).astype(BF16)
        x_send(2, p, U3, SB, 1)
        x_send(1, p, D3, DA, 1)

    ways = ((2 + 12 * c, 14 - 12 * c), (1, 15), (15, 1))

    def owned(p):
        x_arrived(1, p, DB, 0)
        x_arrived(1, p, DA, 1)
        x_arrived(2, p, SA, 0)
        x_arrived(2, p, SB, 1)
        for cols, first, second in ((slice(0, 128), DA, SA), (slice(128, 256), DB, SB)):
            more = first[p].astype(F32) + second[p].astype(F32)
            R[p, :, :, :, cols] = R[p, :, :, :, cols] + more.reshape(4, 4, 16, 128)
        for i, (k, _) in enumerate(ways):
            QA[p, i] = R[p, :, rem(z + k, 4)].astype(BF16)
            send(QA.at[p, i], QR.at[p, i], qs.at[p, i], qr.at[p, i], to_z(k))

    def fourth(p):
        sums = R[p, :, rem(z, 4)]
        for i, (_, k) in enumerate(ways):
            arrived(QR.at[p, i], qs.at[p, i], qr.at[p, i], to_z(k))
            sums = sums + QR[p, i].astype(F32)
        T[p] = sums
        far(p)

    def far(p):
        for m in (2, 1, 3):
            mine = T.at[p, rem(lax.div(z, 4) + m, 4)]
            send(mine, TR.at[p, m - 1], ts.at[p, m - 1], tr.at[p, m - 1], to_z(4 * m))

    def complete(p):
        sums = T[p, lax.div(z, 4)]
        for m in (1, 2, 3):
            arrived(TR.at[p, m - 1], ts.at[p, m - 1], tr.at[p, m - 1], to_z(16 - 4 * m))
            sums = sums + TR[p, m - 1]
        wg_out[:, 256 * p : 256 * p + 256] = sums

    def terms_last():
        out = dot(GT[...].reshape(1024, 1024), H[:, 768:1024])
        AZ[...] = out.reshape(4, 4, 4, 16, 256)
        for i, (k, _) in enumerate(ways):
            QB[i] = AZ[:, :, rem(z + k, 4)].astype(BF16)
            send(QB.at[i], QC.at[i], qbs.at[i], qbr.at[i], to_z(k))

    left, right = slice(0, 128), slice(128, 256)

    def zx_send(i, value):
        ZS[i] = value.astype(BF16)
        send(ZS.at[i], ZR.at[i], zxs.at[i], zxr.at[i], to_x(1 if i % 2 == 0 else 3))

    def zx_arrived(i):
        arrived(ZR.at[i], zxs.at[i], zxr.at[i], to_x(3 if i % 2 == 0 else 1))
        return ZR[i].astype(F32)

    def last_near():
        sums = AZ[:, :, rem(z, 4)]
        for i, (_, k) in enumerate(ways):
            arrived(QC.at[i], qbs.at[i], qbr.at[i], to_z(k))
            sums = sums + QC[i].astype(F32)
        Y[...] = sums
        zx_send(0, Y[rem(x + 2, NX), :, :, left])
        zx_send(1, Y[rem(x + 2, NX), :, :, right])
        zx_send(2, Y[rem(x + 1, NX), :, :, right])
        zx_send(3, Y[rem(x + 3, NX), :, :, left])

    def last_relay():
        zx_send(4, Y[rem(x + 1, NX), :, :, left] + zx_arrived(0))
        zx_send(5, Y[rem(x + 3, NX), :, :, right] + zx_arrived(1))

    def last_owned():
        T[3, :, :, left] = Y[x, :, :, left] + zx_arrived(3) + zx_arrived(4)
        T[3, :, :, right] = Y[x, :, :, right] + zx_arrived(2) + zx_arrived(5)
        far(3)

    def unflip(r, _):
        rows = pl.ds(pl.multiple_of(r * 256, 256), 256)
        G[rows, :] = GT[:, :, rows].reshape(1024, 256).T
        return 0

    def backward(n):
        here = pl.ds(256 * n, 256)
        GH[:, here] = dot(G[...], W[:, :, here].reshape(1024, 256))

    def entered(j):
        part = pl.ds(128 * j, 128)
        normed = X[part, :].astype(F32) * inv_c[part, :]
        inner = jnp.sum(gain[...] * GH[part, :] * normed, axis=1, keepdims=True)
        IN[mp, j : j + 1, :] = to_row(inner)

    def gain_terms_last():
        sums = jnp.sum((W[:, :, 768:1024].astype(F32) * AZ[...].reshape(64, 16, 256)).reshape(1024, 256), axis=0, keepdims=True)
        sums = sums / gain[:, 768:1024]
        GX[x, 6:7, :] = sums[:, left]
        GX[x, 7:8, :] = sums[:, right]

    def gain_terms(p):
        for h, kept in enumerate(((V.at[p, 0], F1, S2.at[p, 0], D3), (V.at[p, 1], D1, S2.at[p, 1], F3))):
            b = 2 * p + h
            cols = pl.ds(128 * b, 128)
            sums = jnp.zeros((1, 128), F32)
            for k, ref in enumerate(kept):
                term = (ref[p] if k % 2 else ref[...]).astype(F32)
                rows = W[pl.ds(16 * rem(x + k, NX), 16), :, cols].astype(F32)
                sums = sums + jnp.sum((rows * term).reshape(256, 128), axis=0, keepdims=True)
            GX[x, b : b + 1, :] = sums / gain[:, cols]

    def w_place(i, j, m):
        there = rem(x + i, NX) * NZ + rem(z + NZ + (0, 1, 2 - 4 * c, -1)[j] + 4 * m, NZ)
        W[there] = WR[i, j, m]

    def column(r, i):
        return to_col(picked[:, 256 * r + 128 * i : 256 * r + 128 * i + 128].astype(F32))

    def choose(r):
        ids = jnp.concatenate([column(r, 0), column(r, 1)], axis=0).astype(jnp.int32)
        slot = lax.broadcasted_iota(jnp.int32, (256, 1), 0) + 256 * r
        ids = jnp.where(slot < count[0], ids, -1)
        number = lax.broadcasted_iota(jnp.int32, (256, 1024), 1)
        H[pl.ds(256 * r, 256), :] = jnp.where(ids == number, 1.0, 0.0).astype(BF16)

    across = pl.ds(1, 3)

    def last_cross(i):
        w_arrived(6 + i, (0, near[i][0], later))
        w_cross(22 + 4 * i, near[i][0], later, most)

    terms_last()
    terms(0)
    w_relayed(10, 0, 0)
    terms(1)
    w_relay(18, 0, later)
    w_relayed(14, pl.ds(1, 3), 0)
    terms(2)
    relay(0)
    w_relayed(18, 0, later)
    for i, (j, k) in enumerate(near):
        w_send(34 + i, (across, 0, later), (across, j, later), to_z(k), rest)
    relay(1)
    last_cross(0)
    last_near()
    relay(2)
    last_cross(1)
    lax.fori_loop(0, 4, unflip, 0)
    owned(0)
    last_relay()
    last_cross(2)
    for j in range(4):
        for m in range(4):
            w_place(0, j, m)
            if j == 0 or m == 0:
                for i in (1, 2, 3):
                    w_place(i, j, m)
    owned(1)
    fourth(0)
    last_owned()
    w_relay(22, near[0][0], later, most)
    for r in range(4):
        choose(r)
    w_relay(26, near[1][0], later, most)
    w_relay(30, near[2][0], later, most)
    owned(2)
    fourth(1)
    for i, (j, k) in enumerate(near):
        w_arrived(34 + i, (across, j, later), rest)
    for i, (j, k) in enumerate(near):
        w_relayed(22 + 4 * i, j, later, most)
    for j in (1, 2, 3):
        for m in (1, 2, 3):
            for i in (1, 2, 3):
                w_place(i, j, m)
    for p in range(3):
        gain_terms(p)
    gain_terms_last()
    for k in range(1, NX):
        send(GX.at[x], GX.at[x], gxs.at[k], gxr.at[k], to_x(k))
    backward(0)
    fourth(2)
    backward(1)
    backward(2)
    backward(3)
    for j in range(8):
        entered(j)
    for k in range(1, 8):
        send(IN.at[mp], IN.at[mp], ins.at[k], inr.at[k], to_mp(k))
    for k in range(1, NX):
        arrived(GX.at[rem(x + NX - k, NX)], gxs.at[k], gxr.at[k], to_x(NX - k))
    GZ[z] = GX[0] + GX[1] + GX[2] + GX[3]
    for k in sorted(range(1, NZ), key=lambda k: abs(k - 8)):
        send(GZ.at[z], GZ.at[z], gzs.at[k], gzr.at[k], to_z(k))
    complete(0)
    complete(3)
    complete(1)
    wait_sends()
    for k in range(1, 8):
        arrived(IN.at[rem(mp + 8 - k, 8)], ins.at[k], inr.at[k], to_mp(8 - k))
    total = IN[0]
    for k in range(1, 8):
        total = total + IN[k]
    IN[8] = total / D

    def finish(j, _):
        rows = pl.ds(pl.multiple_of(j * 128, 128), 128)
        inner = to_col(IN[8, pl.ds(j, 1), :])
        inverse = inv_c[rows, :]
        normed = X[rows, :].astype(F32) * inverse
        RG[rows, :] = (inverse * (gain[...] * GH[rows, :] - normed * inner)).astype(BF16)
        return 0

    lax.fori_loop(0, 8, finish, 0)

    def place(n):
        here = pl.ds(256 * n, 256)
        OUT[:, here] = dot(H[...], RG[:, here]).astype(BF16)
        copy = pltpu.make_async_copy(OUT.at[:, here], rows_out.at[:, here], osem.at[n])
        copy.start()
        return copy

    written = [place(r) for r in range(4)]
    complete(2)
    for k in range(1, NZ):
        arrived(GZ.at[rem(z + NZ - k, NZ)], gzs.at[k], gzr.at[k], to_z(NZ - k))
    total = GZ[0]
    for k in range(1, NZ):
        total = total + GZ[k]
    gg_out[...] = total
    for copy in written:
        copy.wait()
    wait_sends()


def deliver(rows_in, wg_in, gg_in, rows_out, wg_out, gg_out, rows, wg, gg, sem):
    def move(i, src, by, dst):
        return (
            pltpu.make_async_copy(src, by, sem.at[0, i]),
            pltpu.make_async_copy(by, dst, sem.at[1, i]),
        )

    moves = [
        move(i, *(ref.at[pl.ds(128 * i, 128)] for ref in (rows_in, rows, rows_out))) for i in range(8)
    ]
    moves += [move(8, wg_in, wg, wg_out), move(9, gg_in, gg, gg_out)]
    for first, _ in moves:
        first.start()
    for first, second in moves:
        first.wait()
        second.start()
    for _, second in moves:
        second.wait()


def shards(checkpoint, key_grads, key_weight, norm_gain, picked_rows, row_counts):
    any_space = pl.BlockSpec(memory_space=pl.ANY)
    vmem = pl.BlockSpec(memory_space=pltpu.VMEM)
    dma = pltpu.SemaphoreType.DMA
    piece = (4, 16, 16, 128)
    scratch = [
        pltpu.VMEM((1024, 1024), BF16),
        pltpu.VMEM((1024, 128), BF16),
        pltpu.VMEM((8, 128, 1024), BF16),
        pltpu.VMEM((1024, 1024), BF16),
        pltpu.VMEM((NX, 4, 4, 16, 1024), BF16),
        pltpu.VMEM((NX * NZ, 16, 1024), BF16),
        pltpu.VMEM((1024, 1024), BF16),
        pltpu.VMEM((1024, 1024), F32),
        pltpu.VMEM((1024, 1024), BF16),
        pltpu.VMEM((1024, 1024), BF16),
        pltpu.VMEM((1, 1024), F32),
        pltpu.VMEM((1, 1024), jnp.int32),
        pltpu.SMEM((1,), jnp.int32),
        pltpu.VMEM((1024, 1), F32),
        pltpu.VMEM((9, 8, 128), F32),
        pltpu.VMEM((9, 8, 128), F32),
        pltpu.VMEM((NX, 8, 128), F32),
        pltpu.VMEM((NZ, 8, 128), F32),
        pltpu.VMEM((4, 2, 16, 16, 128), BF16),
        pltpu.VMEM(piece, BF16),
        pltpu.VMEM(piece, BF16),
        pltpu.VMEM(piece, F32),
        pltpu.VMEM(piece, F32),
        pltpu.VMEM((4, 2, 16, 16, 128), F32),
        pltpu.VMEM(piece, BF16),
        pltpu.VMEM(piece, BF16),
        pltpu.VMEM((4, 4, 4, 16, 256), F32),
        *[pltpu.VMEM(piece, BF16) for _ in range(6)],
        pltpu.VMEM((4, 3, 4, 16, 256), BF16),
        pltpu.VMEM((4, 3, 4, 16, 256), BF16),
        pltpu.VMEM((4, 4, 16, 256), F32),
        pltpu.VMEM((4, 3, 16, 256), F32),
        pltpu.VMEM((4, 4, 4, 16, 256), F32),
        pltpu.VMEM((3, 4, 4, 16, 256), BF16),
        pltpu.VMEM((3, 4, 4, 16, 256), BF16),
        pltpu.VMEM((4, 4, 16, 256), F32),
        pltpu.VMEM((6, 4, 16, 128), BF16),
        pltpu.VMEM((6, 4, 16, 128), BF16),
        dma((6,)), dma((4,)),
        dma((37,)), dma((37,)),
        dma((10,)), dma((10,)),
        dma((8,)), dma((8,)),
        dma((8,)), dma((8,)),
        dma((NX,)), dma((NX,)),
        dma((NZ,)), dma((NZ,)),
        dma((3, 4, 2)), dma((3, 4, 2)),
        dma((4, 3)), dma((4, 3)),
        dma((4, 3)), dma((4, 3)),
        dma((3,)), dma((3,)),
        dma((6,)), dma((6,)),
    ]
    row_grads, weight_grad, gain_grad = pl.pallas_call(
        kernel,
        out_shape=(
            jax.ShapeDtypeStruct((1024, 1024), BF16),
            jax.ShapeDtypeStruct((16, 1024), F32),
            jax.ShapeDtypeStruct((8, 128), F32),
        ),
        in_specs=[any_space] * 6,
        out_specs=(any_space, vmem, vmem),
        scratch_shapes=scratch,
        compiler_params=pltpu.CompilerParams(
            collective_id=0, has_side_effects=True, vmem_limit_bytes=60 * 1024 * 1024
        ),
        cost_estimate=pl.CostEstimate(flops=6 * 1024**3, bytes_accessed=8 * 1024**2, transcendentals=1024),
        name="norm_key_backward",
    )(checkpoint, key_grads, key_weight, norm_gain.reshape(1, 1024), picked_rows, row_counts)
    row_grads, weight_grad, gain_grad = pl.pallas_call(
        deliver,
        out_shape=(
            jax.ShapeDtypeStruct((1024, 1024), BF16),
            jax.ShapeDtypeStruct((16, 1024), F32),
            jax.ShapeDtypeStruct((8, 128), F32),
        ),
        in_specs=[any_space] * 3,
        out_specs=(any_space,) * 3,
        scratch_shapes=[
            pltpu.VMEM((1024, 1024), BF16),
            pltpu.VMEM((16, 1024), F32),
            pltpu.VMEM((8, 128), F32),
            dma((2, 10)),
        ],
        compiler_params=pltpu.CompilerParams(vmem_limit_bytes=60 * 1024 * 1024),
        name="deliver",
    )(row_grads, weight_grad, gain_grad)
    return row_grads, weight_grad, gain_grad.reshape(1024)


def solution(mesh):
    in_specs = (P("dp", "mp"), P("dp", "mp"), P("dp", "mp"), P("mp"), P("dp", None), P("dp"))
    out_specs = (P("dp", "mp"), P("dp", "mp"), P("mp"))
    return jax.shard_map(shards, mesh=mesh, in_specs=in_specs, out_specs=out_specs, check_vma=False)
```

```python
import functools

import jax
import jax.numpy as jnp
from jax import lax
from jax.experimental import pallas as pl
from jax.experimental.pallas import tpu as pltpu
from jax.sharding import PartitionSpec as P

D = 8192
EPS = 1e-05
NX, NZ, NY = 4, 16, 4
MESH = pl.DeviceIdType.MESH
F32, BF16 = jnp.float32, jnp.bfloat16


def rem(a, n):
    return lax.rem(a, n)


def dot(a, b):
    return jnp.dot(a, b, preferred_element_type=F32)


def kernel(
    x_in, kg_in, w_in, gain_in, picked_in, count_in,
    rows_out, wg_out, gg_out,
    X, KG, GT, G, WR, W, H, GH, RG, OUT,
    gain, picked, count, inv_c,
    SQ, IN, GX, GZ,
    S2, D1, D3, F1, F3, V, U1, U3, R,
    RA, RB, DA, DB, SA, SB, QA, QR, T, TR,
    AZ, QB, QC, Y, ZS, ZR,
    hello, hello_far, lsem, osem, ws, wr, ys, yr, sqs, sqr, ins, inr, gxs, gxr, gzs, gzr,
    xs, xr, qs, qr, ts, tr, qbs, qbr, zxs, zxr,
):
    dp, mp = lax.axis_index("dp"), lax.axis_index("mp")
    x, z = lax.div(dp, NZ), rem(dp, NZ)
    y, c = lax.div(mp, 2), rem(mp, 2)
    pending = []

    def to_x(k):
        return (rem(x + k, NX) * NZ + z, mp)

    def to_z(k):
        return (x * NZ + rem(z + k, NZ), mp)

    def to_y(k):
        return (dp, rem(y + k, NY) * 2 + c)

    def to_mp(k):
        return (dp, rem(mp + k, 8))

    sibling = (dp, 2 * y + 1 - c)

    def send(src, dst, ss, rs, dev):
        copy = pltpu.make_async_remote_copy(
            src_ref=src, dst_ref=dst, send_sem=ss, recv_sem=rs, device_id=dev, device_id_type=MESH
        )
        copy.start()
        pending.append(copy)

    def arrived(dst, ss, rs, dev):
        pltpu.make_async_remote_copy(
            src_ref=dst, dst_ref=dst, send_sem=ss, recv_sem=rs, device_id=dev, device_id_type=MESH
        ).wait_recv()

    def wait_sends():
        while pending:
            pending.pop().wait_send()

    get_kg = pltpu.make_async_copy(kg_in, KG, lsem.at[0])
    get_x = pltpu.make_async_copy(x_in, X, lsem.at[1])
    get_w = pltpu.make_async_copy(w_in, WR.at[0, 0, 0], lsem.at[2])
    get_gain = pltpu.make_async_copy(gain_in, gain, lsem.at[3])
    get_picked = pltpu.make_async_copy(picked_in, picked, lsem.at[4])
    get_count = pltpu.make_async_copy(count_in, count, lsem.at[5])
    get_kg.start()
    get_w.start()
    get_x.start()
    get_gain.start()
    get_picked.start()
    get_count.start()

    barrier = pltpu.get_barrier_semaphore()
    for k in (2, 14, 1, 15):
        pl.semaphore_signal(barrier, inc=1, device_id=to_z(k), device_id_type=MESH)
    for k in range(1, NX):
        pl.semaphore_signal(barrier, inc=1, device_id=to_x(k), device_id_type=MESH)
    for k in range(1, 8):
        pl.semaphore_signal(barrier, inc=1, device_id=to_mp(k), device_id_type=MESH)

    get_kg.wait()

    def flip(j, _):
        rows = pl.ds(pl.multiple_of(j * 128, 128), 128)
        GT[mp, :, rows] = KG[rows, :].T
        return 0

    lax.fori_loop(0, 8, flip, 0)
    get_w.wait()
    pl.semaphore_wait(barrier, 7 + NX - 1 + 4)
    for k in (2, 14):
        pl.semaphore_signal(hello, inc=1, device_id=to_z(k), device_id_type=MESH)

    whole, most, rest = pl.ds(0, 1024), pl.ds(0, 512), pl.ds(512, 512)
    later = pl.ds(1, 3)

    def w_send(i, src, dst, dev, cols=whole):
        send(WR.at[(*src, slice(None), cols)], WR.at[(*dst, slice(None), cols)], ws.at[i], wr.at[i], dev)

    def w_arrived(i, dst, cols=whole):
        arrived(WR.at[(*dst, slice(None), cols)], ws.at[i], wr.at[i], to_x(1))

    near = ((1, 15), (3, 1), (2, 14 - 12 * c))

    def w_cross(i, j, m, cols=whole):
        w_send(i, (0, j, m), (1, j, m), to_x(3), cols)
        w_send(i + 1, (0, j, m), (3, j, m), to_x(1), cols)

    def halves(cols):
        size = cols.size // 2
        return pl.ds(0, size), pl.ds(size, size)

    def w_relay(i, j, m, cols=whole):
        low, high = halves(cols)
        w_arrived(i, (1, j, m), cols)
        w_send(i + 2, (1, j, m), (2, j, m), to_x(3), low)
        w_arrived(i + 1, (3, j, m), cols)
        w_send(i + 3, (3, j, m), (2, j, m), to_x(1), high)

    def w_relayed(i, j, m, cols=whole):
        low, high = halves(cols)
        w_arrived(i + 2, (2, j, m), low)
        w_arrived(i + 3, (2, j, m), high)

    for i, (j, k) in enumerate(near):
        w_send(i, (0, 0, 0), (0, j, 0), to_z(k))
    w_cross(10, 0, 0)

    def block(k, other=False):
        return rem(y + k, NY) * 2 + ((1 - c) if other else c)

    def half(b, h):
        return GT.at[b, pl.ds(64 * h, 64), :]

    send(half(mp, 0), half(mp, 0), ys.at[1], yr.at[1], to_y(1))
    send(half(mp, 1), half(mp, 1), ys.at[3], yr.at[3], to_y(3))
    send(half(mp, 1), half(mp, 1), ys.at[2], yr.at[2], to_y(1))
    send(half(mp, 0), half(mp, 0), ys.at[4], yr.at[4], to_y(3))
    send(GT.at[mp], GT.at[mp], ys.at[0], yr.at[0], sibling)

    eye = lax.broadcasted_iota(jnp.int32, (128, 128), 0) == lax.broadcasted_iota(
        jnp.int32, (128, 128), 1
    )

    def to_row(col):
        return jnp.sum(jnp.where(eye, col, 0.0), axis=0, keepdims=True)

    def to_col(row):
        return jnp.sum(jnp.where(eye, row, 0.0), axis=1, keepdims=True)

    get_x.wait()

    def squares(j, _):
        rows = X[pl.ds(pl.multiple_of(j * 128, 128), 128), :].astype(F32)
        SQ[mp, pl.ds(j, 1), :] = to_row(jnp.sum(rows * rows, axis=1, keepdims=True))
        return 0

    lax.fori_loop(0, 8, squares, 0)
    for k in range(1, 8):
        send(SQ.at[mp], SQ.at[mp], sqs.at[k], sqr.at[k], to_mp(k))

    pl.semaphore_wait(hello, 2)
    for k in (4, 12):
        pl.semaphore_signal(hello_far, inc=1, device_id=to_z(k), device_id_type=MESH)
    for m in (1, 3):
        w_send(2 + m, (0, 0, 0), (0, 0, m), to_z(16 - 4 * m))

    get_picked.wait()
    get_count.wait()
    get_gain.wait()
    live = lax.broadcasted_iota(jnp.int32, (1, 1024), 1) < count[0]
    wanted = jnp.where(live, picked[...], -1)

    def selected(j, _):
        number = lax.broadcasted_iota(jnp.int32, (128, 1024), 0) + j * 128
        hit = jnp.where(wanted == number, 1.0, 0.0)
        inv_c[pl.ds(pl.multiple_of(j * 128, 128), 128), :] = jnp.sum(hit, axis=1, keepdims=True)
        return 0

    lax.fori_loop(0, 8, selected, 0)

    pl.semaphore_wait(hello_far, 2)
    w_send(4, (0, 0, 0), (0, 0, 2), to_z(8))

    for i, (j, k) in enumerate(near):
        w_arrived(i, (0, j, 0))
    w_cross(14, pl.ds(1, 3), 0)
    w_relay(10, 0, 0)

    arrived(half(block(3), 0), ys.at[1], yr.at[1], to_y(3))
    send(half(block(3), 0), half(block(3), 0), ys.at[5], yr.at[5], to_y(1))
    arrived(half(block(1), 1), ys.at[3], yr.at[3], to_y(1))
    send(half(block(1), 1), half(block(1), 1), ys.at[6], yr.at[6], to_y(3))
    for k in range(1, 8):
        arrived(SQ.at[rem(mp + 8 - k, 8)], sqs.at[k], sqr.at[k], to_mp(8 - k))
    total = SQ[0]
    for k in range(1, 8):
        total = total + SQ[k]
    SQ[8] = lax.rsqrt(total / D + EPS)

    def hidden(j, _):
        rows = pl.ds(pl.multiple_of(j * 128, 128), 128)
        inverse = to_col(SQ[8, pl.ds(j, 1), :]) * inv_c[rows, :]
        inv_c[rows, :] = inverse
        normed = X[rows, :].astype(F32) * inverse
        H[rows, :] = (normed * gain[...]).astype(BF16)
        return 0

    lax.fori_loop(0, 8, hidden, 0)
    arrived(half(block(3), 1), ys.at[2], yr.at[2], to_y(3))
    send(GT.at[block(3)], GT.at[block(3)], ys.at[7], yr.at[7], sibling)
    arrived(half(block(1), 0), ys.at[4], yr.at[4], to_y(1))
    send(GT.at[block(1)], GT.at[block(1)], ys.at[8], yr.at[8], sibling)

    for m in (1, 3, 2):
        w_arrived(2 + m, (0, 0, m))
    for i, (j, k) in enumerate(near):
        w_send(6 + i, (0, 0, later), (0, j, later), to_z(k))
    w_cross(18, 0, later)
    w_relay(14, pl.ds(1, 3), 0)
    arrived(half(block(2), 0), ys.at[5], yr.at[5], to_y(3))
    arrived(half(block(2), 1), ys.at[6], yr.at[6], to_y(1))
    send(GT.at[block(2)], GT.at[block(2)], ys.at[9], yr.at[9], sibling)
    arrived(GT.at[block(0, True)], ys.at[0], yr.at[0], sibling)
    arrived(GT.at[block(3, True)], ys.at[7], yr.at[7], sibling)
    arrived(GT.at[block(1, True)], ys.at[8], yr.at[8], sibling)
    arrived(GT.at[block(2, True)], ys.at[9], yr.at[9], sibling)

    def x_send(i, p, src, dst, d):
        send(src.at[p], dst.at[p], xs.at[i, p, d], xr.at[i, p, d], to_x(1 if d == 0 else 3))

    def x_arrived(i, p, dst, d):
        arrived(dst.at[p], xs.at[i, p, d], xr.at[i, p, d], to_x(3 if d == 0 else 1))

    def terms(p):
        def product(k):
            b = rem(x + k, NX)
            lhs = GT[pl.ds(2 * b, 2)].reshape(256, 1024)
            out = dot(lhs, H[:, 256 * p : 256 * p + 256])
            return out[:, :128].reshape(16, 16, 128), out[:, 128:].reshape(16, 16, 128)

        left, right = product(2)
        S2[p, 0] = left.astype(BF16)
        S2[p, 1] = right.astype(BF16)
        send(S2.at[p, 0], RA.at[p], xs.at[0, p, 0], xr.at[0, p, 0], to_x(1))
        send(S2.at[p, 1], RB.at[p], xs.at[0, p, 1], xr.at[0, p, 1], to_x(3))
        left, right = product(1)
        F1[p] = left
        D1[p] = right.astype(BF16)
        left, right = product(3)
        D3[p] = left.astype(BF16)
        F3[p] = right
        left, right = product(0)
        V[p, 0] = left
        V[p, 1] = right
        R[p, :, :, :, :128] = left.reshape(4, 4, 16, 128)
        R[p, :, :, :, 128:] = right.reshape(4, 4, 16, 128)

    def relay(p):
        x_arrived(0, p, RA, 0)
        U1[p] = (F1[p] + RA[p].astype(F32)).astype(BF16)
        x_send(2, p, U1, SA, 0)
        x_send(1, p, D1, DB, 0)
        x_arrived(0, p, RB, 1)
        U3[p] = (F3[p] + RB[p].astype(F32)).astype(BF16)
        x_send(2, p, U3, SB, 1)
        x_send(1, p, D3, DA, 1)

    ways = ((2 + 12 * c, 14 - 12 * c), (1, 15), (15, 1))

    def owned(p):
        x_arrived(1, p, DB, 0)
        x_arrived(1, p, DA, 1)
        x_arrived(2, p, SA, 0)
        x_arrived(2, p, SB, 1)
        for cols, first, second in ((slice(0, 128), DA, SA), (slice(128, 256), DB, SB)):
            more = first[p].astype(F32) + second[p].astype(F32)
            R[p, :, :, :, cols] = R[p, :, :, :, cols] + more.reshape(4, 4, 16, 128)
        for i, (k, _) in enumerate(ways):
            QA[p, i] = R[p, :, rem(z + k, 4)].astype(BF16)
            send(QA.at[p, i], QR.at[p, i], qs.at[p, i], qr.at[p, i], to_z(k))

    def fourth(p):
        sums = R[p, :, rem(z, 4)]
        for i, (_, k) in enumerate(ways):
            arrived(QR.at[p, i], qs.at[p, i], qr.at[p, i], to_z(k))
            sums = sums + QR[p, i].astype(F32)
        T[p] = sums
        far(p)

    def far(p):
        for m in (2, 1, 3):
            mine = T.at[p, rem(lax.div(z, 4) + m, 4)]
            send(mine, TR.at[p, m - 1], ts.at[p, m - 1], tr.at[p, m - 1], to_z(4 * m))

    def complete(p):
        sums = T[p, lax.div(z, 4)]
        for m in (1, 2, 3):
            arrived(TR.at[p, m - 1], ts.at[p, m - 1], tr.at[p, m - 1], to_z(16 - 4 * m))
            sums = sums + TR[p, m - 1]
        wg_out[:, 256 * p : 256 * p + 256] = sums

    def terms_last():
        out = dot(GT[...].reshape(1024, 1024), H[:, 768:1024])
        AZ[...] = out.reshape(4, 4, 4, 16, 256)
        for i, (k, _) in enumerate(ways):
            QB[i] = AZ[:, :, rem(z + k, 4)].astype(BF16)
            send(QB.at[i], QC.at[i], qbs.at[i], qbr.at[i], to_z(k))

    left, right = slice(0, 128), slice(128, 256)

    def zx_send(i, value):
        ZS[i] = value.astype(BF16)
        send(ZS.at[i], ZR.at[i], zxs.at[i], zxr.at[i], to_x(1 if i % 2 == 0 else 3))

    def zx_arrived(i):
        arrived(ZR.at[i], zxs.at[i], zxr.at[i], to_x(3 if i % 2 == 0 else 1))
        return ZR[i].astype(F32)

    def last_near():
        sums = AZ[:, :, rem(z, 4)]
        for i, (_, k) in enumerate(ways):
            arrived(QC.at[i], qbs.at[i], qbr.at[i], to_z(k))
            sums = sums + QC[i].astype(F32)
        Y[...] = sums
        zx_send(0, Y[rem(x + 2, NX), :, :, left])
        zx_send(1, Y[rem(x + 2, NX), :, :, right])
        zx_send(2, Y[rem(x + 1, NX), :, :, right])
        zx_send(3, Y[rem(x + 3, NX), :, :, left])

    def last_relay():
        zx_send(4, Y[rem(x + 1, NX), :, :, left] + zx_arrived(0))
        zx_send(5, Y[rem(x + 3, NX), :, :, right] + zx_arrived(1))

    def last_owned():
        T[3, :, :, left] = Y[x, :, :, left] + zx_arrived(3) + zx_arrived(4)
        T[3, :, :, right] = Y[x, :, :, right] + zx_arrived(2) + zx_arrived(5)
        far(3)

    def unflip(r, _):
        rows = pl.ds(pl.multiple_of(r * 256, 256), 256)
        G[rows, :] = GT[:, :, rows].reshape(1024, 256).T
        return 0

    def backward(n):
        here = pl.ds(256 * n, 256)
        GH[:, here] = dot(G[...], W[:, :, here].reshape(1024, 256))

    def entered(j):
        part = pl.ds(128 * j, 128)
        normed = X[part, :].astype(F32) * inv_c[part, :]
        inner = jnp.sum(gain[...] * GH[part, :] * normed, axis=1, keepdims=True)
        IN[mp, j : j + 1, :] = to_row(inner)

    def gain_terms_last():
        sums = jnp.sum((W[:, :, 768:1024].astype(F32) * AZ[...].reshape(64, 16, 256)).reshape(1024, 256), axis=0, keepdims=True)
        sums = sums / gain[:, 768:1024]
        GX[x, 6:7, :] = sums[:, left]
        GX[x, 7:8, :] = sums[:, right]

    def gain_terms(p):
        for h, kept in enumerate(((V.at[p, 0], F1, S2.at[p, 0], D3), (V.at[p, 1], D1, S2.at[p, 1], F3))):
            b = 2 * p + h
            cols = pl.ds(128 * b, 128)
            sums = jnp.zeros((1, 128), F32)
            for k, ref in enumerate(kept):
                term = (ref[p] if k % 2 else ref[...]).astype(F32)
                rows = W[pl.ds(16 * rem(x + k, NX), 16), :, cols].astype(F32)
                sums = sums + jnp.sum((rows * term).reshape(256, 128), axis=0, keepdims=True)
            GX[x, b : b + 1, :] = sums / gain[:, cols]

    def w_place(i, j, m):
        there = rem(x + i, NX) * NZ + rem(z + NZ + (0, 1, 2 - 4 * c, -1)[j] + 4 * m, NZ)
        W[there] = WR[i, j, m]

    def column(r, i):
        return to_col(picked[:, 256 * r + 128 * i : 256 * r + 128 * i + 128].astype(F32))

    def choose(r):
        ids = jnp.concatenate([column(r, 0), column(r, 1)], axis=0).astype(jnp.int32)
        slot = lax.broadcasted_iota(jnp.int32, (256, 1), 0) + 256 * r
        ids = jnp.where(slot < count[0], ids, -1)
        number = lax.broadcasted_iota(jnp.int32, (256, 1024), 1)
        H[pl.ds(256 * r, 256), :] = jnp.where(ids == number, 1.0, 0.0).astype(BF16)

    across = pl.ds(1, 3)

    def last_cross(i):
        w_arrived(6 + i, (0, near[i][0], later))
        w_cross(22 + 4 * i, near[i][0], later, most)

    terms_last()
    terms(0)
    w_relayed(10, 0, 0)
    terms(1)
    w_relay(18, 0, later)
    w_relayed(14, pl.ds(1, 3), 0)
    terms(2)
    relay(0)
    w_relayed(18, 0, later)
    for i, (j, k) in enumerate(near):
        w_send(34 + i, (across, 0, later), (across, j, later), to_z(k), rest)
    relay(1)
    last_cross(0)
    last_near()
    relay(2)
    last_cross(1)
    lax.fori_loop(0, 4, unflip, 0)
    owned(0)
    last_relay()
    last_cross(2)
    for j in range(4):
        for m in range(4):
            w_place(0, j, m)
            if j == 0 or m == 0:
                for i in (1, 2, 3):
                    w_place(i, j, m)
    owned(1)
    fourth(0)
    last_owned()
    w_relay(22, near[0][0], later, most)
    for r in range(4):
        choose(r)
    w_relay(26, near[1][0], later, most)
    w_relay(30, near[2][0], later, most)
    owned(2)
    fourth(1)
    for i, (j, k) in enumerate(near):
        w_arrived(34 + i, (across, j, later), rest)
    for i, (j, k) in enumerate(near):
        w_relayed(22 + 4 * i, j, later, most)
    for j in (1, 2, 3):
        for m in (1, 2, 3):
            for i in (1, 2, 3):
                w_place(i, j, m)
    for p in range(3):
        gain_terms(p)
    gain_terms_last()
    for k in range(1, NX):
        send(GX.at[x], GX.at[x], gxs.at[k], gxr.at[k], to_x(k))
    backward(0)
    fourth(2)
    backward(1)
    backward(2)
    backward(3)
    for j in range(8):
        entered(j)
    for k in range(1, 8):
        send(IN.at[mp], IN.at[mp], ins.at[k], inr.at[k], to_mp(k))
    for k in range(1, NX):
        arrived(GX.at[rem(x + NX - k, NX)], gxs.at[k], gxr.at[k], to_x(NX - k))
    GZ[z] = GX[0] + GX[1] + GX[2] + GX[3]
    for k in sorted(range(1, NZ), key=lambda k: abs(k - 8)):
        send(GZ.at[z], GZ.at[z], gzs.at[k], gzr.at[k], to_z(k))
    complete(0)
    complete(3)
    complete(1)
    wait_sends()
    for k in range(1, 8):
        arrived(IN.at[rem(mp + 8 - k, 8)], ins.at[k], inr.at[k], to_mp(8 - k))
    total = IN[0]
    for k in range(1, 8):
        total = total + IN[k]
    IN[8] = total / D

    def finish(j, _):
        rows = pl.ds(pl.multiple_of(j * 128, 128), 128)
        inner = to_col(IN[8, pl.ds(j, 1), :])
        inverse = inv_c[rows, :]
        normed = X[rows, :].astype(F32) * inverse
        RG[rows, :] = (inverse * (gain[...] * GH[rows, :] - normed * inner)).astype(BF16)
        return 0

    lax.fori_loop(0, 8, finish, 0)

    def place(n):
        here = pl.ds(256 * n, 256)
        OUT[:, here] = dot(H[...], RG[:, here]).astype(BF16)
        copy = pltpu.make_async_copy(OUT.at[:, here], rows_out.at[:, here], osem.at[n])
        copy.start()
        return copy

    written = [place(r) for r in range(4)]
    complete(2)
    for k in range(1, NZ):
        arrived(GZ.at[rem(z + NZ - k, NZ)], gzs.at[k], gzr.at[k], to_z(NZ - k))
    total = GZ[0]
    for k in range(1, NZ):
        total = total + GZ[k]
    gg_out[...] = total
    for copy in written:
        copy.wait()
    wait_sends()


def deliver(rows_in, wg_in, gg_in, rows_out, wg_out, gg_out, rows, wg, gg, sem):
    def move(i, src, by, dst):
        return (
            pltpu.make_async_copy(src, by, sem.at[0, i]),
            pltpu.make_async_copy(by, dst, sem.at[1, i]),
        )

    moves = [
        move(i, *(ref.at[pl.ds(128 * i, 128)] for ref in (rows_in, rows, rows_out))) for i in range(8)
    ]
    moves += [move(8, wg_in, wg, wg_out), move(9, gg_in, gg, gg_out)]
    for first, _ in moves:
        first.start()
    for first, second in moves:
        first.wait()
        second.start()
    for _, second in moves:
        second.wait()


def shards(checkpoint, key_grads, key_weight, norm_gain, picked_rows, row_counts):
    any_space = pl.BlockSpec(memory_space=pl.ANY)
    vmem = pl.BlockSpec(memory_space=pltpu.VMEM)
    dma = pltpu.SemaphoreType.DMA
    piece = (4, 16, 16, 128)
    scratch = [
        pltpu.VMEM((1024, 1024), BF16),
        pltpu.VMEM((1024, 128), BF16),
        pltpu.VMEM((8, 128, 1024), BF16),
        pltpu.VMEM((1024, 1024), BF16),
        pltpu.VMEM((NX, 4, 4, 16, 1024), BF16),
        pltpu.VMEM((NX * NZ, 16, 1024), BF16),
        pltpu.VMEM((1024, 1024), BF16),
        pltpu.VMEM((1024, 1024), F32),
        pltpu.VMEM((1024, 1024), BF16),
        pltpu.VMEM((1024, 1024), BF16),
        pltpu.VMEM((1, 1024), F32),
        pltpu.VMEM((1, 1024), jnp.int32),
        pltpu.SMEM((1,), jnp.int32),
        pltpu.VMEM((1024, 1), F32),
        pltpu.VMEM((9, 8, 128), F32),
        pltpu.VMEM((9, 8, 128), F32),
        pltpu.VMEM((NX, 8, 128), F32),
        pltpu.VMEM((NZ, 8, 128), F32),
        pltpu.VMEM((4, 2, 16, 16, 128), BF16),
        pltpu.VMEM(piece, BF16),
        pltpu.VMEM(piece, BF16),
        pltpu.VMEM(piece, F32),
        pltpu.VMEM(piece, F32),
        pltpu.VMEM((4, 2, 16, 16, 128), F32),
        pltpu.VMEM(piece, BF16),
        pltpu.VMEM(piece, BF16),
        pltpu.VMEM((4, 4, 4, 16, 256), F32),
        *[pltpu.VMEM(piece, BF16) for _ in range(6)],
        pltpu.VMEM((4, 3, 4, 16, 256), BF16),
        pltpu.VMEM((4, 3, 4, 16, 256), BF16),
        pltpu.VMEM((4, 4, 16, 256), F32),
        pltpu.VMEM((4, 3, 16, 256), F32),
        pltpu.VMEM((4, 4, 4, 16, 256), F32),
        pltpu.VMEM((3, 4, 4, 16, 256), BF16),
        pltpu.VMEM((3, 4, 4, 16, 256), BF16),
        pltpu.VMEM((4, 4, 16, 256), F32),
        pltpu.VMEM((6, 4, 16, 128), BF16),
        pltpu.VMEM((6, 4, 16, 128), BF16),
        pltpu.SemaphoreType.REGULAR,
        pltpu.SemaphoreType.REGULAR,
        dma((6,)), dma((4,)),
        dma((37,)), dma((37,)),
        dma((10,)), dma((10,)),
        dma((8,)), dma((8,)),
        dma((8,)), dma((8,)),
        dma((NX,)), dma((NX,)),
        dma((NZ,)), dma((NZ,)),
        dma((3, 4, 2)), dma((3, 4, 2)),
        dma((4, 3)), dma((4, 3)),
        dma((4, 3)), dma((4, 3)),
        dma((3,)), dma((3,)),
        dma((6,)), dma((6,)),
    ]
    row_grads, weight_grad, gain_grad = pl.pallas_call(
        kernel,
        out_shape=(
            jax.ShapeDtypeStruct((1024, 1024), BF16),
            jax.ShapeDtypeStruct((16, 1024), F32),
            jax.ShapeDtypeStruct((8, 128), F32),
        ),
        in_specs=[any_space] * 6,
        out_specs=(any_space, vmem, vmem),
        scratch_shapes=scratch,
        compiler_params=pltpu.CompilerParams(
            collective_id=0, has_side_effects=True, vmem_limit_bytes=60 * 1024 * 1024
        ),
        cost_estimate=pl.CostEstimate(flops=6 * 1024**3, bytes_accessed=8 * 1024**2, transcendentals=1024),
        name="norm_key_backward",
    )(checkpoint, key_grads, key_weight, norm_gain.reshape(1, 1024), picked_rows, row_counts)
    row_grads, weight_grad, gain_grad = pl.pallas_call(
        deliver,
        out_shape=(
            jax.ShapeDtypeStruct((1024, 1024), BF16),
            jax.ShapeDtypeStruct((16, 1024), F32),
            jax.ShapeDtypeStruct((8, 128), F32),
        ),
        in_specs=[any_space] * 3,
        out_specs=(any_space,) * 3,
        scratch_shapes=[
            pltpu.VMEM((1024, 1024), BF16),
            pltpu.VMEM((16, 1024), F32),
            pltpu.VMEM((8, 128), F32),
            dma((2, 10)),
        ],
        compiler_params=pltpu.CompilerParams(vmem_limit_bytes=60 * 1024 * 1024),
        name="deliver",
    )(row_grads, weight_grad, gain_grad)
    return row_grads, weight_grad, gain_grad.reshape(1024)


def solution(mesh):
    in_specs = (P("dp", "mp"), P("dp", "mp"), P("dp", "mp"), P("mp"), P("dp", None), P("dp"))
    out_specs = (P("dp", "mp"), P("dp", "mp"), P("mp"))
    return jax.shard_map(shards, mesh=mesh, in_specs=in_specs, out_specs=out_specs, check_vma=False)
```
